1024 devices in a mesh: expert: 16 (over z_hi, y), dp: 64 (over x, z_lo, core).
Axes of the slice: x: 4, y: 4, z: 32 (z_hi: 4, z_lo: 8; z = z_hi * 8 + z_lo), core: 2. Of those that a mesh axis runs over, the one named last changes fastest.
Arguments:
- tokens: bfloat16 [262144, 512], P(('expert', 'dp')), may hold values from -6 to 6
- cotangent: bfloat16 [262144, 512], P(('expert', 'dp')), may hold values from -6 to 6
- gates: float32 [262144], P(('expert', 'dp')), may hold values from 0.1 to 1
- expert_ids: int32 [262144], P(('expert', 'dp')), may hold values from 0 to 31
- slot_ids: int32 [262144], P(('expert', 'dp')), may hold values from -1 to 9, as said below
- w_in: bfloat16 [32, 512, 1024], P('expert'), may hold values from -0.25 to 0.25
- w_out: bfloat16 [32, 1024, 512], P('expert'), may hold values from -0.1875 to 0.1875
Outputs:
- grad_tokens: bfloat16 [262144, 512], P(('expert', 'dp'))
- grad_w_out: float32 [1024, 32, 512], P('dp', 'expert')
The draws below stay inside these ranges and needn't reach their ends.
Inputs may be any that keep to these rules, and one draw needn't show every extreme that they name: slot_ids[t] is the number of earlier tokens of t's group with t's expert if that is under 10, else -1; in every group some expert fills all 10 slots and drops tokens.
All inputs are finite; a program needn't handle non-finite values.
Results may differ from the reference program's by a relative error of at most 0.0057.
Values may be sent and summed in bfloat16 or wider, within the bound.
A program may use at most 32 MiB of HBM per device.

```python
import math
import jax
import jax.numpy as jnp
from jax import lax

D = 512
FF = 1024
GROUP = 256
EXPERTS = 32
CAP = 10
TOKENS = 262144


def route_helper(key):
    ngroups = TOKENS // GROUP
    key_base, key_rank, key_main, key_side = jax.random.split(key, 4)
    base = jax.random.randint(key_base, (ngroups, GROUP), 0, EXPERTS)
    rank = jax.vmap(lambda k: jax.random.permutation(k, GROUP))(jax.random.split(key_rank, ngroups))
    main_hot = jax.random.randint(key_main, (), 0, EXPERTS)
    side_hot = jax.random.randint(key_side, (ngroups, 1), 0, EXPERTS)
    chosen = jnp.where(rank < CAP + 2, main_hot, jnp.where(rank < 2 * CAP + 4, side_hot, base))
    onehot = (chosen[:, :, None] == jnp.arange(EXPERTS)[None, None, :]).astype(jnp.int32)
    position = jnp.sum(jnp.cumsum(onehot, axis=1) * onehot, axis=-1) - 1
    slots = jnp.where(position < CAP, position, -1)
    return (chosen.reshape(TOKENS).astype(jnp.int32), slots.reshape(TOKENS).astype(jnp.int32))


def draw_expert_ids(key, part):
    return route_helper(key)[0]


def draw_slot_ids(key, part):
    return route_helper(key)[1]


def level_of(rng, extent, cuts, smallest, top_value):
    loudness, own = 1.0, jax.random.fold_in(rng, 6)
    for axis_at, blocks in cuts:
        steps = jnp.exp(jax.random.uniform(jax.random.fold_in(own, axis_at), (blocks,), jnp.float32, smallest / len(cuts), top_value / len(cuts)))
        loudness = loudness * jnp.repeat(steps, extent[axis_at] // blocks).reshape([-1 if axis == axis_at else 1 for axis in range(len(extent))])
    return loudness


def centred(own_key, extent, scale, reach, cuts=(), kind=jnp.bfloat16):
    drawn = scale * jax.random.normal(own_key, extent, jnp.float32)
    if cuts:
        drawn = drawn * level_of(own_key, extent, cuts, -0.22, 0.18)
    return jnp.clip(drawn, -reach, reach).astype(kind)


def setup_inputs(seed: int = 0) -> dict:
    streams_of = jax.random.split(jax.random.key(seed), 8)
    return {
        "tokens": centred(streams_of[0], (TOKENS, D), 1.0, 6.0, ((0, 1024),)),
        "cotangent": centred(streams_of[1], (TOKENS, D), 1.0, 6.0, ((0, 1024),)),
        "gates": jnp.clip(jnp.exp(math.log(1.0) - 2.3025851 * jax.random.uniform(streams_of[2], (TOKENS,), jnp.float32) ** level_of(streams_of[2], (TOKENS,), ((0, 1024),), -0.2, 0.2)), 0.1, 1.0),
        "expert_ids": draw_expert_ids(jax.random.fold_in(streams_of[7], 71), 0),
        "slot_ids": draw_slot_ids(jax.random.fold_in(streams_of[7], 71), 0),
        "w_in": centred(streams_of[5], (EXPERTS, D, FF), D ** -0.5, 0.25, ((0, 16),)),
        "w_out": centred(streams_of[6], (EXPERTS, FF, D), FF ** -0.5, 0.1875, ((0, 16),)),
    }


def tables(expert_group, slot_group):
    e_match = expert_group[:, None] == jnp.arange(EXPERTS, dtype=jnp.int32)[None, :]
    c_match = slot_group[:, None] == jnp.arange(CAP, dtype=jnp.int32)[None, :]
    both = e_match[:, :, None] & c_match[:, None, :]
    return both.reshape(GROUP, EXPERTS * CAP).astype(jnp.bfloat16)

def reference(tokens, cotangent, gates, expert_ids, slot_ids, w_in, w_out):
    ngroups = TOKENS // GROUP
    weight_scale = 1.0 / (TOKENS // GROUP * CAP) ** 0.5
    scaled = (cotangent.astype(jnp.float32) * gates[:, None]).astype(jnp.bfloat16)
    experts_g = expert_ids.reshape(ngroups, GROUP).astype(jnp.int32)
    slots_g = slot_ids.reshape(ngroups, GROUP).astype(jnp.int32)

    def spread(items):
        e_grp, s_grp, x_grp, g_grp = items
        table = tables(e_grp, s_grp)
        x_part = jnp.dot(table.T, x_grp, preferred_element_type=jnp.float32).astype(jnp.bfloat16)
        g_part = jnp.dot(table.T, g_grp, preferred_element_type=jnp.float32).astype(jnp.bfloat16)
        return (x_part, g_part)
    x_buf, g_buf = lax.map(spread, (experts_g, slots_g, tokens.reshape(ngroups, GROUP, D), scaled.reshape(ngroups, GROUP, D)))

    def to_expert(buf):
        return buf.reshape(ngroups, EXPERTS, CAP, D).transpose(1, 0, 2, 3).reshape(EXPERTS, ngroups * CAP, D)

    def per_expert(items):
        x_rows, g_rows, w_first, w_second = items
        pre = jnp.dot(x_rows, w_first, preferred_element_type=jnp.float32)
        hidden, pull = jax.vjp(jax.nn.gelu, pre)
        hidden_b = hidden.astype(jnp.bfloat16)
        grad_w = jnp.dot(hidden_b.T, g_rows, preferred_element_type=jnp.float32) * weight_scale
        grad_hidden = jnp.dot(g_rows, w_second.T, preferred_element_type=jnp.float32)
        grad_pre = pull(grad_hidden)[0].astype(jnp.bfloat16)
        grad_rows = jnp.dot(grad_pre, w_first.T, preferred_element_type=jnp.float32).astype(jnp.bfloat16)
        return (grad_w, grad_rows)
    grad_w, grad_buf = lax.map(per_expert, (to_expert(x_buf), to_expert(g_buf), w_in, w_out))
    back = grad_buf.reshape(EXPERTS, ngroups, CAP, D).transpose(1, 0, 2, 3).reshape(ngroups, EXPERTS * CAP, D)

    def collect(items):
        e_grp, s_grp, b_grp = items
        return jnp.dot(tables(e_grp, s_grp), b_grp, preferred_element_type=jnp.float32).astype(jnp.bfloat16)
    grad_tokens = lax.map(collect, (experts_g, slots_g, back)).reshape(TOKENS, D)
    grad_w_out = grad_w.transpose(1, 0, 2)
    return (grad_tokens, grad_w_out)
```

```python
import functools
import math

import jax
import jax.numpy as jnp
from jax import lax
from jax.experimental import pallas as pl
from jax.experimental.pallas import tpu as pltpu
from jax.sharding import PartitionSpec as P

MESH = pl.DeviceIdType.MESH
CAP = 10
F32 = jnp.float32
BF16 = jnp.bfloat16
ZH, Y, X, ZL, C = 4, 4, 4, 8, 2


def nn(a, b):
    return lax.dot_general(a, b, (((1,), (0,)), ((), ())), preferred_element_type=F32)


def nt(a, b):
    return lax.dot_general(a, b, (((1,), (1,)), ((), ())), preferred_element_type=F32)


def tn(a, b):
    return lax.dot_general(a, b, (((0,), (0,)), ((), ())), preferred_element_type=F32)


def one_hot(rows, cols):
    return jnp.where(rows == cols, 1.0, 0.0).astype(BF16)


def kernel(
    dims, scale,
    tok_hbm, cot_hbm, gate_ref, eid_ref, sid_ref, win_hbm, wout_hbm,
    gt_ref, gw_ref,
    tok, cot, win, wout, send, recv, xg32, xg, grow, sback, rback,
    own, csend, crecv, xsend, xrecv, zsend, zrecv,
    in_sem, w_sem, fs, fr, bs, br, cs, cr, xs, xr, zs, zr,
):
    zh_n, y_n, x_n, zl_n, c_n = dims
    n = zh_n * y_n
    tokens, width = tok.shape
    ff = win.shape[2]
    half = width // 2
    quarter = width // 4
    chunk = ff // x_n
    main = 16 * n

    ex = lax.axis_index("expert")
    dp = lax.axis_index("dp")
    zh, yy = ex // y_n, ex % y_n
    xx, zl, core = dp // (zl_n * c_n), (dp // c_n) % zl_n, dp % c_n

    def expert_peer(k):
        to_z = (zh + k // y_n) % zh_n
        to_y = (yy + k % y_n) % y_n
        return to_z * y_n + to_y

    def dp_id(a, b, c):
        return (a * zl_n + b) * c_n + c

    in_copies = [
        pltpu.make_async_copy(tok_hbm, tok, in_sem.at[0]),
        pltpu.make_async_copy(cot_hbm, cot, in_sem.at[1]),
    ]
    w_copies = [
        pltpu.make_async_copy(win_hbm, win, w_sem.at[0]),
        pltpu.make_async_copy(wout_hbm, wout, w_sem.at[1]),
    ]
    for copy in in_copies + w_copies:
        copy.start()

    barrier = pltpu.get_barrier_semaphore()

    def greet(to_e, to_d):
        pl.semaphore_signal(barrier, inc=1, device_id=(to_e, to_d), device_id_type=MESH)

    def greet_expert(k, carry):
        greet(expert_peer(k), dp)
        return carry

    lax.fori_loop(1, n, greet_expert, 0)
    greet(ex, dp_id(xx, zl, 1 - core))
    for k in range(1, x_n):
        greet(ex, dp_id((xx + k) % x_n, zl, core))
    for k in range(1, zl_n):
        greet(ex, dp_id(xx, (zl + k) % zl_n, core))

    slot = sid_ref[...]
    code = jnp.where(slot >= 0, eid_ref[...] * CAP + slot, -1)
    row = lax.broadcasted_iota(jnp.int32, (main, 1), 0)
    main_code = (row // 8) * CAP + row % 8
    tail_block = (row // 4) % 4
    tail_code = (2 * (row // 16) + (row // 2) % 2) * CAP + 8 + row % 2
    t_main = one_hot(main_code, code)
    t_tail = one_hot(tail_code, code)
    gates = gate_ref[...]
    gate_main = jnp.sum(jnp.where(main_code == code, gates, 0.0), axis=1, keepdims=True)
    gate_tail = jnp.sum(jnp.where(tail_code == code, gates, 0.0), axis=1, keepdims=True)

    for copy in in_copies:
        copy.wait()
    send[:, :, :width] = nn(t_main, tok[...]).astype(BF16).reshape(n, 16, width)
    send[:, :, width : 2 * width] = (
        (nn(t_main, cot[...]) * gate_main).astype(BF16).reshape(n, 16, width)
    )
    tail_x = nn(t_tail, tok[...])
    tail_g = nn(t_tail, cot[...]) * gate_tail
    tail = jnp.where(
        tail_block == 0,
        tail_x[:, :half],
        jnp.where(
            tail_block == 1,
            tail_x[:, half:],
            jnp.where(tail_block == 2, tail_g[:, :half], tail_g[:, half:]),
        ),
    )
    send[:, :, 2 * width :] = tail.astype(BF16).reshape(n, 16, half)

    pl.semaphore_wait(barrier, (n - 1) + 1 + (x_n - 1) + (zl_n - 1))

    def forward(to):
        return pltpu.make_async_remote_copy(
            src_ref=send.at[to], dst_ref=recv.at[ex], send_sem=fs.at[to], recv_sem=fr.at[ex],
            device_id=(to, dp), device_id_type=MESH,
        )

    def forward_from(src):
        return pltpu.make_async_remote_copy(
            src_ref=send.at[src], dst_ref=recv.at[src], send_sem=fs.at[src], recv_sem=fr.at[src],
            device_id=(src, dp), device_id_type=MESH,
        )

    def start_forward(k, carry):
        forward(expert_peer(n - k)).start()
        return carry

    lax.fori_loop(1, n, start_forward, 0)
    recv[pl.ds(ex, 1)] = send[pl.ds(ex, 1)]

    def wait_forward(k, carry):
        forward_from(expert_peer(k)).wait_recv()
        return carry

    lax.fori_loop(1, n, wait_forward, 0)

    for s in range(n):
        block = recv[s, :, : 2 * width].astype(F32)
        xg32[0, s * 8 : s * 8 + 8, :] = block[:8]
        xg32[1, s * 8 : s * 8 + 8, :] = block[8:]
    part = 2 * n
    col = lax.broadcasted_iota(jnp.int32, (1, main), 1)
    wanted = (
        ((row // 2) % n) * 16 + ((row // part) % 4) * 4 + (row // (4 * part)) * 2 + row % 2
    )
    tails = nn(one_hot(wanted, col), recv[:, :, 2 * width :].reshape(main, half))
    for a in range(2):
        for q in range(4):
            at = (a * 4 + q) * part
            xg32[a, 8 * n :, q * half : (q + 1) * half] = tails[at : at + part]
    for a in range(2):
        xg[a] = xg32[a].astype(BF16)
    for copy in w_copies:
        copy.wait()
    grow[...] = jnp.zeros_like(grow)

    other = 1 - core

    def to_core(a, to_x):
        return pltpu.make_async_remote_copy(
            src_ref=csend.at[a, to_x], dst_ref=crecv.at[a, to_x],
            send_sem=cs.at[a, to_x], recv_sem=cr.at[a, to_x],
            device_id=(ex, dp_id(xx, zl, other)), device_id_type=MESH,
        )

    k0 = 0.7978845608028654
    k1 = 0.044715

    def expert_chunk(i, carry):
        a = i % 2
        to_x = (xx + 1 + i // 2) % x_n
        f0 = pl.multiple_of(to_x * chunk, chunk)
        xa = xg[a, :, :width]
        ga = xg[a, :, width:]
        w1 = win[a, :, pl.ds(f0, chunk)]
        w2 = wout[a, pl.ds(f0, chunk), :]
        pre = nn(xa, w1)
        grad_hidden = nt(ga, w2)
        square = pre * pre
        th = jnp.tanh(k0 * pre * (1.0 + k1 * square))
        cdf = 0.5 * (1.0 + th)
        hidden = (pre * cdf).astype(BF16)
        slope = cdf + 0.5 * pre * (1.0 - th * th) * (k0 * (1.0 + 3.0 * k1 * square))
        grad_pre = (grad_hidden * slope).astype(BF16)
        grow[a] += nt(grad_pre, w1)
        term = (tn(hidden, ga) * scale).reshape(zl_n, c_n, 16, width)
        even, odd = term[:, 0], term[:, 1]
        mine = core == 0
        own[a, to_x] = jnp.where(mine, even, odd)
        csend[a, to_x] = jnp.where(mine, odd, even).astype(BF16)
        to_core(a, to_x).start()
        return carry

    lax.fori_loop(0, 2 * x_n, expert_chunk, 0)

    for s in range(n):
        both = jnp.concatenate([grow[0, s * 8 : s * 8 + 8, :], grow[1, s * 8 : s * 8 + 8, :]], axis=0)
        sback[s, :, :width] = both.astype(BF16)
    small = jnp.concatenate([grow[0, 8 * n :, :], grow[1, 8 * n :, :]], axis=0).astype(BF16)
    small_col = lax.broadcasted_iota(jnp.int32, (1, 2 * part), 1)
    spread = nn(one_hot(((row // 2) % 2) * part + (row // 16) * 2 + row % 2, small_col), small)
    cols = [spread[:, q * quarter : (q + 1) * quarter] for q in range(4)]
    picked = jnp.where(
        tail_block == 0,
        cols[0],
        jnp.where(tail_block == 1, cols[1], jnp.where(tail_block == 2, cols[2], cols[3])),
    )
    sback[:, :, width:] = picked.astype(BF16).reshape(n, 16, quarter)

    def back_to(to):
        return pltpu.make_async_remote_copy(
            src_ref=sback.at[to], dst_ref=rback.at[ex], send_sem=bs.at[to], recv_sem=br.at[ex],
            device_id=(to, dp), device_id_type=MESH,
        )

    def back_from(src):
        return pltpu.make_async_remote_copy(
            src_ref=sback.at[src], dst_ref=rback.at[src], send_sem=bs.at[src], recv_sem=br.at[src],
            device_id=(src, dp), device_id_type=MESH,
        )

    def start_back(k, carry):
        back_to(expert_peer(n - k)).start()
        return carry

    lax.fori_loop(1, n, start_back, 0)
    rback[pl.ds(ex, 1)] = sback[pl.ds(ex, 1)]

    def to_x_copy(a, to_x):
        return pltpu.make_async_remote_copy(
            src_ref=xsend.at[a, to_x], dst_ref=xrecv.at[a, xx],
            send_sem=xs.at[a, to_x], recv_sem=xr.at[a, xx],
            device_id=(ex, dp_id(to_x, zl, core)), device_id_type=MESH,
        )

    def from_x_copy(a, src):
        return pltpu.make_async_remote_copy(
            src_ref=xsend.at[a, src], dst_ref=xrecv.at[a, src],
            send_sem=xs.at[a, src], recv_sem=xr.at[a, src],
            device_id=(ex, dp_id(src, zl, core)), device_id_type=MESH,
        )

    def pass_x(i, carry):
        a = i % 2
        to_x = (xx + 1 + i // 2) % x_n
        to_core(a, to_x).wait_recv()
        xsend[a, to_x] = (own[a, to_x] + crecv[a, to_x].astype(F32)).astype(BF16)
        to_x_copy(a, to_x).start()
        return carry

    lax.fori_loop(0, 2 * (x_n - 1), pass_x, 0)
    for a in range(2):
        to_core(a, xx).wait_recv()
        own[a, xx] += crecv[a, xx].astype(F32)

    def to_z_copy(a, to_z):
        return pltpu.make_async_remote_copy(
            src_ref=zsend.at[a, to_z], dst_ref=zrecv.at[a, zl],
            send_sem=zs.at[a, to_z], recv_sem=zr.at[a, zl],
            device_id=(ex, dp_id(xx, to_z, core)), device_id_type=MESH,
        )

    def from_z_copy(a, src):
        return pltpu.make_async_remote_copy(
            src_ref=zsend.at[a, src], dst_ref=zrecv.at[a, src],
            send_sem=zs.at[a, src], recv_sem=zr.at[a, src],
            device_id=(ex, dp_id(xx, src, core)), device_id_type=MESH,
        )

    for a in range(2):
        for k in range(1, x_n):
            src = (xx + x_n - k) % x_n
            from_x_copy(a, src).wait_recv()
            own[a, xx] += xrecv[a, src].astype(F32)
        zsend[a] = own[a, xx].astype(BF16)
        for k in range(1, zl_n):
            to_z_copy(a, (zl + k) % zl_n).start()

    def wait_back(k, carry):
        back_from(expert_peer(k)).wait_recv()
        return carry

    lax.fori_loop(1, n, wait_back, 0)
    back_main = rback[:, :, :width].reshape(main, width)
    back_tail = rback[:, :, width:].reshape(main, quarter).astype(F32)
    wide = jnp.concatenate(
        [jnp.where(tail_block == q, back_tail, 0.0) for q in range(4)], axis=1
    ).astype(BF16)
    gt_ref[...] = (tn(t_main, back_main) + tn(t_tail, wide)).astype(BF16)

    for a in range(2):
        total = own[a, xx, zl]
        for k in range(1, zl_n):
            src = (zl + k) % zl_n
            from_z_copy(a, src).wait_recv()
            total = total + zrecv[a, src].astype(F32)
        gw_ref[:, a, :] = total

    def wait_sent(k, carry):
        to = expert_peer(k)
        forward(to).wait_send()
        back_to(to).wait_send()
        return carry

    lax.fori_loop(1, n, wait_sent, 0)
    for a in range(2):
        for k in range(x_n):
            to_core(a, (xx + k) % x_n).wait_send()
        for k in range(1, x_n):
            to_x_copy(a, (xx + k) % x_n).wait_send()
        for k in range(1, zl_n):
            to_z_copy(a, (zl + k) % zl_n).wait_send()


def on_device(dims, tokens, cotangent, gates, expert_ids, slot_ids, w_in, w_out):
    zh_n, y_n, x_n, zl_n, c_n = dims
    n = zh_n * y_n
    rows, width = tokens.shape
    ff = w_in.shape[2]
    scale = 1.0 / math.sqrt(n * x_n * zl_n * c_n * CAP)
    per = 10 * n
    dma = pltpu.SemaphoreType.DMA
    hbm = pl.BlockSpec(memory_space=pl.ANY)
    vmem = pl.BlockSpec(memory_space=pltpu.VMEM)
    return pl.pallas_call(
        functools.partial(kernel, dims, scale),
        out_shape=(
            jax.ShapeDtypeStruct((rows, width), BF16),
            jax.ShapeDtypeStruct((ff // (x_n * zl_n * c_n), 2, width), F32),
        ),
        in_specs=[hbm, hbm, vmem, vmem, vmem, hbm, hbm],
        out_specs=(vmem, vmem),
        scratch_shapes=[
            pltpu.VMEM((rows, width), BF16),
            pltpu.VMEM((rows, width), BF16),
            pltpu.VMEM(w_in.shape, BF16),
            pltpu.VMEM(w_out.shape, BF16),
            pltpu.VMEM((n, 16, 2 * width + width // 2), BF16),
            pltpu.VMEM((n, 16, 2 * width + width // 2), BF16),
            pltpu.VMEM((2, per, 2 * width), F32),
            pltpu.VMEM((2, per, 2 * width), BF16),
            pltpu.VMEM((2, per, width), F32),
            pltpu.VMEM((n, 16, width + width // 4), BF16),
            pltpu.VMEM((n, 16, width + width // 4), BF16),
            pltpu.VMEM((2, x_n, zl_n, 16, width), F32),
            pltpu.VMEM((2, x_n, zl_n, 16, width), BF16),
            pltpu.VMEM((2, x_n, zl_n, 16, width), BF16),
            pltpu.VMEM((2, x_n, zl_n, 16, width), BF16),
            pltpu.VMEM((2, x_n, zl_n, 16, width), BF16),
            pltpu.VMEM((2, zl_n, 16, width), BF16),
            pltpu.VMEM((2, zl_n, 16, width), BF16),
            dma((2,)),
            dma((2,)),
            dma((n,)),
            dma((n,)),
            dma((n,)),
            dma((n,)),
            dma((2, x_n)),
            dma((2, x_n)),
            dma((2, x_n)),
            dma((2, x_n)),
            dma((2, zl_n)),
            dma((2, zl_n)),
        ],
        compiler_params=pltpu.CompilerParams(
            collective_id=0, has_side_effects=True, vmem_limit_bytes=48 << 20
        ),
        cost_estimate=pl.CostEstimate(
            flops=8 * 2 * per * width * ff, bytes_accessed=6 << 20, transcendentals=2 * per * ff
        ),
        name="expert_backward",
    )(
        tokens, cotangent, gates.reshape(1, rows), expert_ids.reshape(1, rows),
        slot_ids.reshape(1, rows), w_in, w_out,
    )


def solution(mesh, dims=(ZH, Y, X, ZL, C)):
    return jax.shard_map(
        functools.partial(on_device, dims),
        mesh=mesh,
        in_specs=(
            P(("expert", "dp"), None),
            P(("expert", "dp"), None),
            P(("expert", "dp")),
            P(("expert", "dp")),
            P(("expert", "dp")),
            P("expert", None, None),
            P("expert", None, None),
        ),
        out_specs=(P(("expert", "dp"), None), P("dp", "expert", None)),
        check_vma=False,
    )
```

```python
import functools
import math

import jax
import jax.numpy as jnp
from jax import lax
from jax.experimental import pallas as pl
from jax.experimental.pallas import tpu as pltpu
from jax.sharding import PartitionSpec as P

MESH = pl.DeviceIdType.MESH
CAP = 10
F32 = jnp.float32
BF16 = jnp.bfloat16
ZH, Y, X, ZL, C = 4, 4, 4, 8, 2


def nn(a, b):
    return lax.dot_general(a, b, (((1,), (0,)), ((), ())), preferred_element_type=F32)


def nt(a, b):
    return lax.dot_general(a, b, (((1,), (1,)), ((), ())), preferred_element_type=F32)


def tn(a, b):
    return lax.dot_general(a, b, (((0,), (0,)), ((), ())), preferred_element_type=F32)


def one_hot(rows, cols):
    return jnp.where(rows == cols, 1.0, 0.0).astype(BF16)


def round_up(rows):
    return (rows + 15) // 16 * 16


def kernel(
    dims, scale,
    tok_hbm, cot_hbm, gate_hbm, eid_hbm, sid_hbm, win_hbm, wout_hbm,
    gt_ref, gw_ref,
    tok, cot, gate, eid, sid, win, wout, send, recv, xg_near, xg_far, tails_in, grow_near, grow_far,
    sback, rback, acc, own, csend, crecv, xsend, xrecv, zsend, zrecv,
    in_sem, w_sem, fs, fr, bs, br, cs, cr, xs, xr, zs, zr,
):
    zh_n, y_n, x_n, zl_n, c_n = dims
    n = zh_n * y_n
    tokens, width = tok.shape
    ff = win.shape[2]
    half = width // 2
    quarter = width // 4
    chunk = ff // x_n
    main = 16 * n

    ex = lax.axis_index("expert")
    dp = lax.axis_index("dp")
    zh, yy = ex // y_n, ex % y_n
    xx, zl, core = dp // (zl_n * c_n), (dp // c_n) % zl_n, dp % c_n
    other = 1 - core

    steps_z = sorted(range(zh_n), key=lambda dz: min(dz, zh_n - dz))
    offsets = [(dz, dy) for dz in steps_z for dy in range(y_n)]
    near = n - y_n

    def peer(k):
        dz, dy = offsets[k]
        return ((zh + dz) % zh_n) * y_n + (yy + dy) % y_n

    def source(k):
        dz, dy = offsets[k]
        return ((zh + zh_n - dz) % zh_n) * y_n + (yy + y_n - dy) % y_n

    def dp_id(a, b, c):
        return (a * zl_n + b) * c_n + c

    in_copies = [
        pltpu.make_async_copy(src, dst, in_sem.at[i])
        for i, (src, dst) in enumerate(
            [(eid_hbm, eid), (sid_hbm, sid), (gate_hbm, gate), (tok_hbm, tok), (cot_hbm, cot)]
        )
    ]
    w_copies = [
        pltpu.make_async_copy(win_hbm, win, w_sem.at[0]),
        pltpu.make_async_copy(wout_hbm, wout, w_sem.at[1]),
    ]
    for copy in in_copies + w_copies:
        copy.start()

    barrier = pltpu.get_barrier_semaphore()

    def greet(to_e, to_d):
        pl.semaphore_signal(barrier, inc=1, device_id=(to_e, to_d), device_id_type=MESH)

    for k in range(1, n):
        greet(peer(k), dp)
    greet(ex, dp_id(xx, zl, other))
    for k in range(1, x_n):
        greet(ex, dp_id((xx + k) % x_n, zl, core))
    for k in range(1, zl_n):
        greet(ex, dp_id(xx, (zl + k) % zl_n, core))

    for copy in in_copies[:3]:
        copy.wait()
    slot = sid[...]
    code = jnp.where(slot >= 0, eid[...] * CAP + slot, -1)
    row = lax.broadcasted_iota(jnp.int32, (main, 1), 0)
    main_code = (row // 8) * CAP + row % 8
    tail_block = (row // 4) % 4
    tail_code = (2 * (row // 16) + (row // 2) % 2) * CAP + 8 + row % 2
    t_main = one_hot(main_code, code)
    t_tail = one_hot(tail_code, code)
    gates = gate[...]
    gate_main = jnp.sum(jnp.where(main_code == code, gates, 0.0), axis=1, keepdims=True)
    gate_tail = jnp.sum(jnp.where(tail_code == code, gates, 0.0), axis=1, keepdims=True)

    for copy in in_copies[3:]:
        copy.wait()
    send[:, :, :width] = nn(t_main, tok[...]).astype(BF16).reshape(n, 16, width)
    send[:, :, width : 2 * width] = (
        (nn(t_main, cot[...]) * gate_main).astype(BF16).reshape(n, 16, width)
    )
    tail_x = nn(t_tail, tok[...])
    tail_g = nn(t_tail, cot[...]) * gate_tail
    tail = jnp.where(
        tail_block == 0,
        tail_x[:, :half],
        jnp.where(
            tail_block == 1,
            tail_x[:, half:],
            jnp.where(tail_block == 2, tail_g[:, :half], tail_g[:, half:]),
        ),
    )
    send[:, :, 2 * width :] = tail.astype(BF16).reshape(n, 16, half)

    pl.semaphore_wait(barrier, (n - 1) + 1 + (x_n - 1) + (zl_n - 1))

    def forward(to):
        return pltpu.make_async_remote_copy(
            src_ref=send.at[to], dst_ref=recv.at[ex], send_sem=fs.at[to], recv_sem=fr.at[ex],
            device_id=(to, dp), device_id_type=MESH,
        )

    def forward_from(src):
        return pltpu.make_async_remote_copy(
            src_ref=send.at[src], dst_ref=recv.at[src], send_sem=fs.at[src], recv_sem=fr.at[src],
            device_id=(src, dp), device_id_type=MESH,
        )

    def back_to(to):
        return pltpu.make_async_remote_copy(
            src_ref=sback.at[to], dst_ref=rback.at[ex], send_sem=bs.at[to], recv_sem=br.at[ex],
            device_id=(to, dp), device_id_type=MESH,
        )

    def back_from(src):
        return pltpu.make_async_remote_copy(
            src_ref=sback.at[src], dst_ref=rback.at[src], send_sem=bs.at[src], recv_sem=br.at[src],
            device_id=(src, dp), device_id_type=MESH,
        )

    for k in range(1, n):
        forward(peer(k)).start()
    recv[pl.ds(ex, 1)] = send[pl.ds(ex, 1)]

    def gather(first, count, xg):
        for k in range(count):
            src = source(first + k)
            block = recv[src, :, : 2 * width].astype(F32)
            xg[0, k * 8 : k * 8 + 8, :] = block[:8]
            xg[1, k * 8 : k * 8 + 8, :] = block[8:]
            tails_in[k * 16 : k * 16 + 16, :] = recv[src, :, 2 * width :]
        part = 2 * count
        r = lax.broadcasted_iota(jnp.int32, (8 * part, 1), 0)
        col = lax.broadcasted_iota(jnp.int32, (1, 8 * part), 1)
        wanted = (
            ((r // 2) % count) * 16
            + ((r // part) % 4) * 4
            + (r // (4 * part)) * 2
            + r % 2
        )
        tails = nn(one_hot(wanted, col), tails_in[: 8 * part, :])
        for a in range(2):
            for q in range(4):
                at = (a * 4 + q) * part
                xg[a, 8 * count : 10 * count, q * half : (q + 1) * half] = tails[at : at + part]
            spare = xg.shape[1] - 10 * count
            if spare:
                xg[a, 10 * count :, :] = jnp.zeros((spare, 2 * width), F32)

    k0 = 0.7978845608028654
    k1 = 0.044715

    def place(i):
        return i % 2, (xx + 1 + i // 2) % x_n

    def multiply(xg, grow, i):
        a, to_x = place(i)
        f0 = pl.multiple_of(to_x * chunk, chunk)
        xa = xg[a, :, :width].astype(BF16)
        ga = xg[a, :, width:].astype(BF16)
        w1 = win[a, :, pl.ds(f0, chunk)]
        w2 = wout[a, pl.ds(f0, chunk), :]
        pre = nn(xa, w1)
        grad_hidden = nt(ga, w2)
        square = pre * pre
        th = jnp.tanh(k0 * pre * (1.0 + k1 * square))
        cdf = 0.5 * (1.0 + th)
        hidden = (pre * cdf).astype(BF16)
        slope = cdf + 0.5 * pre * (1.0 - th * th) * (k0 * (1.0 + 3.0 * k1 * square))
        grad_pre = (grad_hidden * slope).astype(BF16)
        grow[a] += nt(grad_pre, w1)
        return tn(hidden, ga)

    def give_back(first, count, grow):
        for k in range(count):
            both = jnp.concatenate(
                [grow[0, k * 8 : k * 8 + 8, :], grow[1, k * 8 : k * 8 + 8, :]], axis=0
            )
            sback[source(first + k), :, :width] = both.astype(BF16)
        part = 2 * count
        small = jnp.concatenate(
            [grow[0, 8 * count : 10 * count, :], grow[1, 8 * count : 10 * count, :]], axis=0
        ).astype(BF16)
        r = lax.broadcasted_iota(jnp.int32, (16 * count, 1), 0)
        col = lax.broadcasted_iota(jnp.int32, (1, 2 * part), 1)
        spread = nn(one_hot(((r // 2) % 2) * part + (r // 16) * 2 + r % 2, col), small)
        block = (r // 4) % 4
        cols = [spread[:, q * quarter : (q + 1) * quarter] for q in range(4)]
        picked = jnp.where(
            block == 0, cols[0], jnp.where(block == 1, cols[1], jnp.where(block == 2, cols[2], cols[3]))
        ).astype(BF16)
        for k in range(count):
            sback[source(first + k), :, width:] = picked[k * 16 : k * 16 + 16]
            if first + k > 0:
                back_to(source(first + k)).start()

    for k in range(1, near):
        forward_from(source(k)).wait_recv()
    gather(0, near, xg_near)
    for copy in w_copies:
        copy.wait()
    grow_near[...] = jnp.zeros_like(grow_near)
    grow_far[...] = jnp.zeros_like(grow_far)

    def near_chunk(i, carry):
        a, to_x = place(i)
        acc[a, to_x] = multiply(xg_near, grow_near, i).reshape(zl_n, c_n, 16, width)
        return carry

    lax.fori_loop(0, 2 * x_n, near_chunk, 0)
    give_back(0, near, grow_near)
    rback[pl.ds(ex, 1)] = sback[pl.ds(ex, 1)]

    def to_core(a, to_x):
        return pltpu.make_async_remote_copy(
            src_ref=csend.at[a, to_x], dst_ref=crecv.at[a, to_x],
            send_sem=cs.at[a, to_x], recv_sem=cr.at[a, to_x],
            device_id=(ex, dp_id(xx, zl, other)), device_id_type=MESH,
        )

    def to_x_copy(a, to_x):
        return pltpu.make_async_remote_copy(
            src_ref=xsend.at[a, to_x], dst_ref=xrecv.at[a, xx],
            send_sem=xs.at[a, to_x], recv_sem=xr.at[a, xx],
            device_id=(ex, dp_id(to_x, zl, core)), device_id_type=MESH,
        )

    def from_x_copy(a, src):
        return pltpu.make_async_remote_copy(
            src_ref=xsend.at[a, src], dst_ref=xrecv.at[a, src],
            send_sem=xs.at[a, src], recv_sem=xr.at[a, src],
            device_id=(ex, dp_id(src, zl, core)), device_id_type=MESH,
        )

    def to_z_copy(a, to_z):
        return pltpu.make_async_remote_copy(
            src_ref=zsend.at[a, to_z], dst_ref=zrecv.at[a, zl],
            send_sem=zs.at[a, to_z], recv_sem=zr.at[a, zl],
            device_id=(ex, dp_id(xx, to_z, core)), device_id_type=MESH,
        )

    def from_z_copy(a, src):
        return pltpu.make_async_remote_copy(
            src_ref=zsend.at[a, src], dst_ref=zrecv.at[a, src],
            send_sem=zs.at[a, src], recv_sem=zr.at[a, src],
            device_id=(ex, dp_id(xx, src, core)), device_id_type=MESH,
        )

    def far_chunk(i):
        a, to_x = place(i)
        term = (acc[a, to_x] + multiply(xg_far, grow_far, i).reshape(zl_n, c_n, 16, width)) * scale
        even, odd = term[:, 0], term[:, 1]
        mine = core == 0
        own[a, to_x] = jnp.where(mine, even, odd)
        csend[a, to_x] = jnp.where(mine, odd, even).astype(BF16)
        to_core(a, to_x).start()

    def far_first(i, carry):
        far_chunk(i)
        return carry

    def far_next(i, carry):
        far_chunk(i)
        a, to_x = place(i - 2)
        to_core(a, to_x).wait_recv()
        xsend[a, to_x] = (own[a, to_x] + crecv[a, to_x].astype(F32)).astype(BF16)
        to_x_copy(a, to_x).start()
        return carry

    for k in range(near, n):
        forward_from(source(k)).wait_recv()
    gather(near, n - near, xg_far)
    lax.fori_loop(0, 2, far_first, 0)
    lax.fori_loop(2, 2 * x_n, far_next, 0)
    give_back(near, n - near, grow_far)

    for a in range(2):
        to_core(a, xx).wait_recv()
        own[a, xx] += crecv[a, xx].astype(F32)
    for a in range(2):
        for k in range(1, x_n):
            src = (xx + x_n - k) % x_n
            from_x_copy(a, src).wait_recv()
            own[a, xx] += xrecv[a, src].astype(F32)
        zsend[a] = own[a, xx].astype(BF16)
        for k in range(1, zl_n):
            to_z_copy(a, (zl + k) % zl_n).start()

    for k in range(1, n):
        back_from(peer(k)).wait_recv()
    back_main = rback[:, :, :width].reshape(main, width)
    back_tail = rback[:, :, width:].reshape(main, quarter).astype(F32)
    wide = jnp.concatenate(
        [jnp.where(tail_block == q, back_tail, 0.0) for q in range(4)], axis=1
    ).astype(BF16)
    gt_ref[...] = (tn(t_main, back_main) + tn(t_tail, wide)).astype(BF16)

    for a in range(2):
        total = own[a, xx, zl]
        for k in range(1, zl_n):
            src = (zl + k) % zl_n
            from_z_copy(a, src).wait_recv()
            total = total + zrecv[a, src].astype(F32)
        gw_ref[:, a, :] = total

    for k in range(1, n):
        forward(peer(k)).wait_send()
        back_to(source(k)).wait_send()
    for a in range(2):
        for k in range(x_n):
            to_core(a, (xx + k) % x_n).wait_send()
        for k in range(1, x_n):
            to_x_copy(a, (xx + k) % x_n).wait_send()
        for k in range(1, zl_n):
            to_z_copy(a, (zl + k) % zl_n).wait_send()


def on_device(dims, tokens, cotangent, gates, expert_ids, slot_ids, w_in, w_out):
    zh_n, y_n, x_n, zl_n, c_n = dims
    n = zh_n * y_n
    rows, width = tokens.shape
    ff = w_in.shape[2]
    scale = 1.0 / math.sqrt(n * x_n * zl_n * c_n * CAP)
    per = 10 * n
    near = n - y_n
    near_rows, far_rows = round_up(10 * near), round_up(10 * y_n)
    dma = pltpu.SemaphoreType.DMA
    hbm = pl.BlockSpec(memory_space=pltpu.HBM)
    vmem = pl.BlockSpec(memory_space=pltpu.VMEM)
    return pl.pallas_call(
        functools.partial(kernel, dims, scale),
        out_shape=(
            jax.ShapeDtypeStruct((rows, width), BF16),
            jax.ShapeDtypeStruct((ff // (x_n * zl_n * c_n), 2, width), F32),
        ),
        in_specs=[hbm] * 7,
        out_specs=(vmem, vmem),
        scratch_shapes=[
            pltpu.VMEM((rows, width), BF16),
            pltpu.VMEM((rows, width), BF16),
            pltpu.VMEM((1, rows), F32),
            pltpu.VMEM((1, rows), jnp.int32),
            pltpu.VMEM((1, rows), jnp.int32),
            pltpu.VMEM(w_in.shape, BF16),
            pltpu.VMEM(w_out.shape, BF16),
            pltpu.VMEM((n, 16, 2 * width + width // 2), BF16),
            pltpu.VMEM((n, 16, 2 * width + width // 2), BF16),
            pltpu.VMEM((2, near_rows, 2 * width), F32),
            pltpu.VMEM((2, far_rows, 2 * width), F32),
            pltpu.VMEM((16 * max(near, y_n), width // 2), BF16),
            pltpu.VMEM((2, near_rows, width), F32),
            pltpu.VMEM((2, far_rows, width), F32),
            pltpu.VMEM((n, 16, width + width // 4), BF16),
            pltpu.VMEM((n, 16, width + width // 4), BF16),
            pltpu.VMEM((2, x_n, zl_n, c_n, 16, width), F32),
            pltpu.VMEM((2, x_n, zl_n, 16, width), F32),
            pltpu.VMEM((2, x_n, zl_n, 16, width), BF16),
            pltpu.VMEM((2, x_n, zl_n, 16, width), BF16),
            pltpu.VMEM((2, x_n, zl_n, 16, width), BF16),
            pltpu.VMEM((2, x_n, zl_n, 16, width), BF16),
            pltpu.VMEM((2, zl_n, 16, width), BF16),
            pltpu.VMEM((2, zl_n, 16, width), BF16),
            dma((5,)),
            dma((2,)),
            dma((n,)),
            dma((n,)),
            dma((n,)),
            dma((n,)),
            dma((2, x_n)),
            dma((2, x_n)),
            dma((2, x_n)),
            dma((2, x_n)),
            dma((2, zl_n)),
            dma((2, zl_n)),
        ],
        compiler_params=pltpu.CompilerParams(
            collective_id=0, has_side_effects=True, vmem_limit_bytes=48 << 20
        ),
        cost_estimate=pl.CostEstimate(
            flops=8 * 2 * per * width * ff, bytes_accessed=6 << 20, transcendentals=2 * per * ff
        ),
        name="expert_backward",
    )(
        tokens, cotangent, gates.reshape(1, rows), expert_ids.reshape(1, rows),
        slot_ids.reshape(1, rows), w_in, w_out,
    )


def solution(mesh, dims=(ZH, Y, X, ZL, C)):
    return jax.shard_map(
        functools.partial(on_device, dims),
        mesh=mesh,
        in_specs=(
            P(("expert", "dp"), None),
            P(("expert", "dp"), None),
            P(("expert", "dp")),
            P(("expert", "dp")),
            P(("expert", "dp")),
            P("expert", None, None),
            P("expert", None, None),
        ),
        out_specs=(P(("expert", "dp"), None), P("dp", "expert", None)),
        check_vma=False,
    )
```

```python
import functools
import math

import jax
import jax.numpy as jnp
from jax import lax
from jax.experimental import pallas as pl
from jax.experimental.pallas import tpu as pltpu
from jax.sharding import PartitionSpec as P

MESH = pl.DeviceIdType.MESH
CAP = 10
F32 = jnp.float32
BF16 = jnp.bfloat16
ZH, Y, X, ZL, C = 4, 4, 4, 8, 2


def nn(a, b):
    return lax.dot_general(a, b, (((1,), (0,)), ((), ())), preferred_element_type=F32)


def nt(a, b):
    return lax.dot_general(a, b, (((1,), (1,)), ((), ())), preferred_element_type=F32)


def tn(a, b):
    return lax.dot_general(a, b, (((0,), (0,)), ((), ())), preferred_element_type=F32)


def one_hot(rows, cols):
    return jnp.where(rows == cols, 1.0, 0.0).astype(BF16)


def round_up(rows):
    return (rows + 15) // 16 * 16


def kernel(
    dims, scale,
    tok_hbm, cot_hbm, gate_hbm, eid_hbm, sid_hbm, win_hbm, wout_hbm,
    gt_ref, gw_ref,
    tok, cot, gate, eid, sid, win, wout, send, recv, xg_near, xg_far, tails_in, grow_near, grow_far,
    sback, rback, acc, own, csend, crecv, xsend, xrecv, zsend, zrecv,
    in_sem, w_sem, fs, fr, bs, br, cs, cr, xs, xr, zs, zr,
):
    zh_n, y_n, x_n, zl_n, c_n = dims
    n = zh_n * y_n
    tokens, width = tok.shape
    ff = win.shape[2]
    half = width // 2
    quarter = width // 4
    chunk = ff // x_n
    main = 16 * n

    ex = lax.axis_index("expert")
    dp = lax.axis_index("dp")
    zh, yy = ex // y_n, ex % y_n
    xx, zl, core = dp // (zl_n * c_n), (dp // c_n) % zl_n, dp % c_n
    other = 1 - core

    steps_z = sorted(range(zh_n), key=lambda dz: min(dz, zh_n - dz))
    offsets = [(dz, dy) for dz in steps_z for dy in range(y_n)]
    near = n - y_n

    def peer(k):
        dz, dy = offsets[k]
        return ((zh + dz) % zh_n) * y_n + (yy + dy) % y_n

    def source(k):
        dz, dy = offsets[k]
        return ((zh + zh_n - dz) % zh_n) * y_n + (yy + y_n - dy) % y_n

    def dp_id(a, b, c):
        return (a * zl_n + b) * c_n + c

    in_copies = [
        pltpu.make_async_copy(src, dst, in_sem.at[i])
        for i, (src, dst) in enumerate(
            [(eid_hbm, eid), (sid_hbm, sid), (gate_hbm, gate), (tok_hbm, tok), (cot_hbm, cot)]
        )
    ]
    w_copies = [
        pltpu.make_async_copy(win_hbm, win, w_sem.at[0]),
        pltpu.make_async_copy(wout_hbm, wout, w_sem.at[1]),
    ]
    for copy in in_copies + w_copies:
        copy.start()

    barrier = pltpu.get_barrier_semaphore()

    def greet(to_e, to_d):
        pl.semaphore_signal(barrier, inc=1, device_id=(to_e, to_d), device_id_type=MESH)

    for k in range(1, n):
        greet(peer(k), dp)
    greet(ex, dp_id(xx, zl, other))
    for k in range(1, x_n):
        greet(ex, dp_id((xx + k) % x_n, zl, core))
    for k in range(1, zl_n):
        greet(ex, dp_id(xx, (zl + k) % zl_n, core))

    for copy in in_copies[:3]:
        copy.wait()
    slot = sid[...]
    code = jnp.where(slot >= 0, eid[...] * CAP + slot, -1)
    row = lax.broadcasted_iota(jnp.int32, (main, 1), 0)
    main_code = (row // 8) * CAP + row % 8
    tail_block = (row // 4) % 4
    tail_code = (2 * (row // 16) + (row // 2) % 2) * CAP + 8 + row % 2
    t_main = one_hot(main_code, code)
    t_tail = one_hot(tail_code, code)
    gates = gate[...]
    gate_main = jnp.sum(jnp.where(main_code == code, gates, 0.0), axis=1, keepdims=True)
    gate_tail = jnp.sum(jnp.where(tail_code == code, gates, 0.0), axis=1, keepdims=True)

    for copy in in_copies[3:]:
        copy.wait()
    send[:, :, :width] = nn(t_main, tok[...]).astype(BF16).reshape(n, 16, width)
    send[:, :, width : 2 * width] = (
        (nn(t_main, cot[...]) * gate_main).astype(BF16).reshape(n, 16, width)
    )
    tail_x = nn(t_tail, tok[...])
    tail_g = nn(t_tail, cot[...]) * gate_tail
    tail = jnp.where(
        tail_block == 0,
        tail_x[:, :half],
        jnp.where(
            tail_block == 1,
            tail_x[:, half:],
            jnp.where(tail_block == 2, tail_g[:, :half], tail_g[:, half:]),
        ),
    )
    send[:, :, 2 * width :] = tail.astype(BF16).reshape(n, 16, half)

    pl.semaphore_wait(barrier, (n - 1) + 1 + (x_n - 1) + (zl_n - 1))

    def forward(to):
        return pltpu.make_async_remote_copy(
            src_ref=send.at[to], dst_ref=recv.at[ex], send_sem=fs.at[to], recv_sem=fr.at[ex],
            device_id=(to, dp), device_id_type=MESH,
        )

    def forward_from(src):
        return pltpu.make_async_remote_copy(
            src_ref=send.at[src], dst_ref=recv.at[src], send_sem=fs.at[src], recv_sem=fr.at[src],
            device_id=(src, dp), device_id_type=MESH,
        )

    def back_to(to):
        return pltpu.make_async_remote_copy(
            src_ref=sback.at[to], dst_ref=rback.at[ex], send_sem=bs.at[to], recv_sem=br.at[ex],
            device_id=(to, dp), device_id_type=MESH,
        )

    def back_from(src):
        return pltpu.make_async_remote_copy(
            src_ref=sback.at[src], dst_ref=rback.at[src], send_sem=bs.at[src], recv_sem=br.at[src],
            device_id=(src, dp), device_id_type=MESH,
        )

    for k in range(1, n):
        forward(peer(k)).start()
    recv[pl.ds(ex, 1)] = send[pl.ds(ex, 1)]

    def gather(first, count, xg):
        for k in range(count):
            src = source(first + k)
            block = recv[src, :, : 2 * width].astype(F32)
            xg[0, k * 8 : k * 8 + 8, :] = block[:8]
            xg[1, k * 8 : k * 8 + 8, :] = block[8:]
            tails_in[k * 16 : k * 16 + 16, :] = recv[src, :, 2 * width :]
        part = 2 * count
        r = lax.broadcasted_iota(jnp.int32, (8 * part, 1), 0)
        col = lax.broadcasted_iota(jnp.int32, (1, 8 * part), 1)
        wanted = (
            ((r // 2) % count) * 16
            + ((r // part) % 4) * 4
            + (r // (4 * part)) * 2
            + r % 2
        )
        tails = nn(one_hot(wanted, col), tails_in[: 8 * part, :])
        for a in range(2):
            for q in range(4):
                at = (a * 4 + q) * part
                xg[a, 8 * count : 10 * count, q * half : (q + 1) * half] = tails[at : at + part]
            spare = xg.shape[1] - 10 * count
            if spare:
                xg[a, 10 * count :, :] = jnp.zeros((spare, 2 * width), F32)

    k0 = 0.7978845608028654
    k1 = 0.044715

    def place(i):
        return i % 2, (xx + 1 + i // 2) % x_n

    def multiply(xg, grow, i):
        a, to_x = place(i)
        f0 = pl.multiple_of(to_x * chunk, chunk)
        xa = xg[a, :, :width].astype(BF16)
        ga = xg[a, :, width:].astype(BF16)
        w1 = win[a, :, pl.ds(f0, chunk)]
        w2 = wout[a, pl.ds(f0, chunk), :]
        pre = nn(xa, w1)
        grad_hidden = nt(ga, w2)
        square = pre * pre
        th = jnp.tanh(k0 * pre * (1.0 + k1 * square))
        cdf = 0.5 * (1.0 + th)
        hidden = (pre * cdf).astype(BF16)
        slope = cdf + 0.5 * pre * (1.0 - th * th) * (k0 * (1.0 + 3.0 * k1 * square))
        grad_pre = (grad_hidden * slope).astype(BF16)
        grow[a] += nt(grad_pre, w1)
        return tn(hidden, ga)

    def give_back(first, count, grow):
        for k in range(count):
            both = jnp.concatenate(
                [grow[0, k * 8 : k * 8 + 8, :], grow[1, k * 8 : k * 8 + 8, :]], axis=0
            )
            sback[source(first + k), :, :width] = both.astype(BF16)
        part = 2 * count
        small = jnp.concatenate(
            [grow[0, 8 * count : 10 * count, :], grow[1, 8 * count : 10 * count, :]], axis=0
        ).astype(BF16)
        r = lax.broadcasted_iota(jnp.int32, (16 * count, 1), 0)
        col = lax.broadcasted_iota(jnp.int32, (1, 2 * part), 1)
        spread = nn(one_hot(((r // 2) % 2) * part + (r // 16) * 2 + r % 2, col), small)
        block = (r // 4) % 4
        cols = [spread[:, q * quarter : (q + 1) * quarter] for q in range(4)]
        picked = jnp.where(
            block == 0, cols[0], jnp.where(block == 1, cols[1], jnp.where(block == 2, cols[2], cols[3]))
        ).astype(BF16)
        for k in range(count):
            sback[source(first + k), :, width:] = picked[k * 16 : k * 16 + 16]
            if first + k > 0:
                back_to(source(first + k)).start()

    for k in range(1, near):
        forward_from(source(k)).wait_recv()
    gather(0, near, xg_near)
    for copy in w_copies:
        copy.wait()
    grow_near[...] = jnp.zeros_like(grow_near)
    grow_far[...] = jnp.zeros_like(grow_far)

    def near_chunk(i, carry):
        a, to_x = place(i)
        acc[a, to_x] = multiply(xg_near, grow_near, i).reshape(zl_n, c_n, 16, width)
        return carry

    lax.fori_loop(0, 2 * x_n, near_chunk, 0)
    give_back(0, near, grow_near)
    rback[pl.ds(ex, 1)] = sback[pl.ds(ex, 1)]

    def to_core(a, to_x):
        return pltpu.make_async_remote_copy(
            src_ref=csend.at[a, to_x], dst_ref=crecv.at[a, to_x],
            send_sem=cs.at[a, to_x], recv_sem=cr.at[a, to_x],
            device_id=(ex, dp_id(xx, zl, other)), device_id_type=MESH,
        )

    def to_x_copy(a, to_x):
        return pltpu.make_async_remote_copy(
            src_ref=xsend.at[a, to_x], dst_ref=xrecv.at[a, xx],
            send_sem=xs.at[a, to_x], recv_sem=xr.at[a, xx],
            device_id=(ex, dp_id(to_x, zl, core)), device_id_type=MESH,
        )

    def from_x_copy(a, src):
        return pltpu.make_async_remote_copy(
            src_ref=xsend.at[a, src], dst_ref=xrecv.at[a, src],
            send_sem=xs.at[a, src], recv_sem=xr.at[a, src],
            device_id=(ex, dp_id(src, zl, core)), device_id_type=MESH,
        )

    def to_z_copy(a, to_z):
        return pltpu.make_async_remote_copy(
            src_ref=zsend.at[a, to_z], dst_ref=zrecv.at[a, zl],
            send_sem=zs.at[a, to_z], recv_sem=zr.at[a, zl],
            device_id=(ex, dp_id(xx, to_z, core)), device_id_type=MESH,
        )

    def from_z_copy(a, src):
        return pltpu.make_async_remote_copy(
            src_ref=zsend.at[a, src], dst_ref=zrecv.at[a, src],
            send_sem=zs.at[a, src], recv_sem=zr.at[a, src],
            device_id=(ex, dp_id(xx, src, core)), device_id_type=MESH,
        )

    def far_chunk(i):
        a, to_x = place(i)
        term = (acc[a, to_x] + multiply(xg_far, grow_far, i).reshape(zl_n, c_n, 16, width)) * scale
        even, odd = term[:, 0], term[:, 1]
        mine = core == 0
        own[a, to_x] = jnp.where(mine, even, odd)
        csend[a, to_x] = jnp.where(mine, odd, even).astype(BF16)
        to_core(a, to_x).start()

    def far_first(i, carry):
        far_chunk(i)
        return carry

    def far_next(i, carry):
        far_chunk(i)
        a, to_x = place(i - 2)
        to_core(a, to_x).wait_recv()
        xsend[a, to_x] = (own[a, to_x] + crecv[a, to_x].astype(F32)).astype(BF16)
        to_x_copy(a, to_x).start()
        return carry

    for k in range(near, n):
        forward_from(source(k)).wait_recv()
    gather(near, n - near, xg_far)
    lax.fori_loop(0, 2, far_first, 0)
    lax.fori_loop(2, 2 * x_n, far_next, 0)
    give_back(near, n - near, grow_far)

    for a in range(2):
        to_core(a, xx).wait_recv()
        own[a, xx] += crecv[a, xx].astype(F32)
    for a in range(2):
        for k in range(1, x_n):
            src = (xx + x_n - k) % x_n
            from_x_copy(a, src).wait_recv()
            own[a, xx] += xrecv[a, src].astype(F32)
        zsend[a] = own[a, xx].astype(BF16)
        for k in range(1, zl_n):
            to_z_copy(a, (zl + k) % zl_n).start()

    for k in range(1, n):
        back_from(peer(k)).wait_recv()
    back_main = rback[:, :, :width].reshape(main, width)
    back_tail = rback[:, :, width:].reshape(main, quarter).astype(F32)
    wide = jnp.concatenate(
        [jnp.where(tail_block == q, back_tail, 0.0) for q in range(4)], axis=1
    ).astype(BF16)
    gt_ref[...] = (tn(t_main, back_main) + tn(t_tail, wide)).astype(BF16)

    for a in range(2):
        total = own[a, xx, zl]
        for k in range(1, zl_n):
            src = (zl + k) % zl_n
            from_z_copy(a, src).wait_recv()
            total = total + zrecv[a, src].astype(F32)
        gw_ref[:, a, :] = total

    for k in range(1, n):
        forward(peer(k)).wait_send()
        back_to(source(k)).wait_send()
    for a in range(2):
        for k in range(x_n):
            to_core(a, (xx + k) % x_n).wait_send()
        for k in range(1, x_n):
            to_x_copy(a, (xx + k) % x_n).wait_send()
        for k in range(1, zl_n):
            to_z_copy(a, (zl + k) % zl_n).wait_send()


def on_device(dims, tokens, cotangent, gates, expert_ids, slot_ids, w_in, w_out):
    zh_n, y_n, x_n, zl_n, c_n = dims
    n = zh_n * y_n
    rows, width = tokens.shape
    ff = w_in.shape[2]
    scale = 1.0 / math.sqrt(n * x_n * zl_n * c_n * CAP)
    per = 10 * n
    near = n - y_n
    near_rows, far_rows = round_up(10 * near), round_up(10 * y_n)
    dma = pltpu.SemaphoreType.DMA
    hbm = pl.BlockSpec(memory_space=pltpu.HBM)
    vmem = pl.BlockSpec(memory_space=pltpu.VMEM)
    return pl.pallas_call(
        functools.partial(kernel, dims, scale),
        out_shape=(
            jax.ShapeDtypeStruct((rows, width), BF16),
            jax.ShapeDtypeStruct((ff // (x_n * zl_n * c_n), 2, width), F32),
        ),
        in_specs=[hbm] * 7,
        out_specs=(vmem, vmem),
        scratch_shapes=[
            pltpu.VMEM((rows, width), BF16),
            pltpu.VMEM((rows, width), BF16),
            pltpu.VMEM((1, rows), F32),
            pltpu.VMEM((1, rows), jnp.int32),
            pltpu.VMEM((1, rows), jnp.int32),
            pltpu.VMEM(w_in.shape, BF16),
            pltpu.VMEM(w_out.shape, BF16),
            pltpu.VMEM((n, 16, 2 * width + width // 2), BF16),
            pltpu.VMEM((n, 16, 2 * width + width // 2), BF16),
            pltpu.VMEM((2, near_rows, 2 * width), F32),
            pltpu.VMEM((2, far_rows, 2 * width), F32),
            pltpu.VMEM((16 * max(near, y_n), width // 2), BF16),
            pltpu.VMEM((2, near_rows, width), F32),
            pltpu.VMEM((2, far_rows, width), F32),
            pltpu.VMEM((n, 16, width + width // 4), BF16),
            pltpu.VMEM((n, 16, width + width // 4), BF16),
            pltpu.VMEM((2, x_n, zl_n, c_n, 16, width), F32),
            pltpu.VMEM((2, x_n, zl_n, 16, width), F32),
            pltpu.VMEM((2, x_n, zl_n, 16, width), BF16),
            pltpu.VMEM((2, x_n, zl_n, 16, width), BF16),
            pltpu.VMEM((2, x_n, zl_n, 16, width), BF16),
            pltpu.VMEM((2, x_n, zl_n, 16, width), BF16),
            pltpu.VMEM((2, zl_n, 16, width), BF16),
            pltpu.VMEM((2, zl_n, 16, width), BF16),
            dma((5,)),
            dma((2,)),
            dma((n,)),
            dma((n,)),
            dma((n,)),
            dma((n,)),
            dma((2, x_n)),
            dma((2, x_n)),
            dma((2, x_n)),
            dma((2, x_n)),
            dma((2, zl_n)),
            dma((2, zl_n)),
        ],
        compiler_params=pltpu.CompilerParams(
            collective_id=0, has_side_effects=True, vmem_limit_bytes=60 << 20
        ),
        cost_estimate=pl.CostEstimate(
            flops=8 * 2 * per * width * ff, bytes_accessed=6 << 20, transcendentals=2 * per * ff
        ),
        name="expert_backward",
    )(
        tokens, cotangent, gates.reshape(1, rows), expert_ids.reshape(1, rows),
        slot_ids.reshape(1, rows), w_in, w_out,
    )


def solution(mesh, dims=(ZH, Y, X, ZL, C)):
    return jax.shard_map(
        functools.partial(on_device, dims),
        mesh=mesh,
        in_specs=(
            P(("expert", "dp"), None),
            P(("expert", "dp"), None),
            P(("expert", "dp")),
            P(("expert", "dp")),
            P(("expert", "dp")),
            P("expert", None, None),
            P("expert", None, None),
        ),
        out_specs=(P(("expert", "dp"), None), P("dp", "expert", None)),
        check_vma=False,
    )
```

```python
import functools
import math

import jax
import jax.numpy as jnp
from jax import lax
from jax.experimental import pallas as pl
from jax.experimental.pallas import tpu as pltpu
from jax.sharding import PartitionSpec as P

MESH = pl.DeviceIdType.MESH
CAP = 10
F32 = jnp.float32
BF16 = jnp.bfloat16
ZH, Y, X, ZL, C = 4, 4, 4, 8, 2


def nn(a, b):
    return lax.dot_general(a, b, (((1,), (0,)), ((), ())), preferred_element_type=F32)


def nt(a, b):
    return lax.dot_general(a, b, (((1,), (1,)), ((), ())), preferred_element_type=F32)


def tn(a, b):
    return lax.dot_general(a, b, (((0,), (0,)), ((), ())), preferred_element_type=F32)


def one_hot(rows, cols):
    return jnp.where(rows == cols, 1.0, 0.0).astype(BF16)


def round_up(rows):
    return (rows + 15) // 16 * 16


def kernel(
    dims, scale,
    tok_hbm, cot_hbm, gate_hbm, eid_hbm, sid_hbm, win_hbm, wout_hbm,
    gt_ref, gw_ref,
    tok, cot, gate, eid, sid, win, wout, send, recv, xg_near, xg_far, tails_in, grow_near, grow_far,
    sback, rback, dsend, drecv, tsend, trecv, acc, xsend, xrecv, zsend, zrecv,
    in_sem, w_sem, fs, fr, bs, br, ds, dr, xs, xr, zs, zr,
):
    zh_n, y_n, x_n, zl_n, c_n = dims
    n = zh_n * y_n
    width = tok.shape[1]
    ff = win.shape[1]
    quarter = width // 4
    chunk = ff // x_n
    experts = c_n * n

    ex = lax.axis_index("expert")
    dp = lax.axis_index("dp")
    zh, yy = ex // y_n, ex % y_n
    xx, zl, core = dp // (zl_n * c_n), (dp // c_n) % zl_n, dp % c_n
    other = 1 - core
    here = ex * c_n + core

    steps_z = sorted(range(zh_n), key=lambda dz: min(dz, zh_n - dz))
    offsets = [(dz, dy) for dz in steps_z for dy in range(y_n)]
    near = n - y_n

    def peer(k):
        dz, dy = offsets[k]
        return ((zh + dz) % zh_n) * y_n + (yy + dy) % y_n

    def source(k):
        dz, dy = offsets[k]
        return ((zh + zh_n - dz) % zh_n) * y_n + (yy + y_n - dy) % y_n

    def dp_id(a, b, c):
        return (a * zl_n + b) * c_n + c

    levels = zl_n.bit_length() - 1

    def z_bit(level):
        return (zl // 2**level) % 2

    def z_partner(level):
        return zl + 2**level * (1 - 2 * z_bit(level))

    in_copies = [
        pltpu.make_async_copy(src, dst, in_sem.at[i])
        for i, (src, dst) in enumerate(
            [(eid_hbm, eid), (sid_hbm, sid), (gate_hbm, gate), (tok_hbm, tok), (cot_hbm, cot)]
        )
    ]
    w_copies = [
        pltpu.make_async_copy(win_hbm.at[core], win, w_sem.at[0]),
        pltpu.make_async_copy(wout_hbm.at[core], wout, w_sem.at[1]),
    ]
    for copy in in_copies + w_copies:
        copy.start()

    barrier = pltpu.get_barrier_semaphore()

    def greet(to_e, to_d):
        pl.semaphore_signal(barrier, inc=1, device_id=(to_e, to_d), device_id_type=MESH)

    for k in range(n):
        greet(peer(k), dp_id(xx, zl, other))
        if k > 0:
            greet(peer(k), dp)
    for k in range(1, x_n):
        greet(ex, dp_id((xx + k) % x_n, zl, core))
    for level in range(levels):
        greet(ex, dp_id(xx, z_partner(level), core))
    greet(ex, dp_id(xx, z_partner(levels - 1), other))

    for copy in in_copies[:3]:
        copy.wait()
    slot = sid[...]
    code = jnp.where(slot >= 0, eid[...] * CAP + slot, -1)
    row = lax.broadcasted_iota(jnp.int32, (8 * experts, 1), 0)
    main_code = (row // 8) * CAP + row % 8
    trow = lax.broadcasted_iota(jnp.int32, (16 * experts, 1), 0)
    tail_code = (trow // 16) * CAP + 8 + trow % 2
    t_main = one_hot(main_code, code)
    t_tail = one_hot(tail_code, code)
    gates = gate[...]
    gate_main = jnp.sum(jnp.where(main_code == code, gates, 0.0), axis=1, keepdims=True)
    gate_tail = jnp.sum(jnp.where(tail_code == code, gates, 0.0), axis=1, keepdims=True)

    for copy in in_copies[3:]:
        copy.wait()
    main_x = nn(t_main, tok[...]).reshape(experts, 8, width)
    main_g = (nn(t_main, cot[...]) * gate_main).reshape(experts, 8, width)
    send[:, :, :width] = jnp.concatenate([main_x, main_g], axis=1).astype(BF16)
    tail_x = nn(t_tail, tok[...])
    tail_g = nn(t_tail, cot[...]) * gate_tail
    block = (trow // 2) % 8
    tail = tail_x[:, :quarter]
    for q in range(1, 8):
        part = tail_x if q < 4 else tail_g
        at = (q % 4) * quarter
        tail = jnp.where(block == q, part[:, at : at + quarter], tail)
    send[:, :, width:] = tail.astype(BF16).reshape(experts, 16, quarter)

    pl.semaphore_wait(barrier, (n * c_n - 1) + (x_n - 1) + levels + 1)

    def forward(to, to_c):
        return pltpu.make_async_remote_copy(
            src_ref=send.at[to * c_n + to_c], dst_ref=recv.at[here],
            send_sem=fs.at[to * c_n + to_c], recv_sem=fr.at[here],
            device_id=(to, dp_id(xx, zl, to_c)), device_id_type=MESH,
        )

    def forward_from(src, src_c):
        at = src * c_n + src_c
        return pltpu.make_async_remote_copy(
            src_ref=send.at[at], dst_ref=recv.at[at], send_sem=fs.at[at], recv_sem=fr.at[at],
            device_id=(src, dp_id(xx, zl, src_c)), device_id_type=MESH,
        )

    def back_to(to):
        return pltpu.make_async_remote_copy(
            src_ref=sback.at[to], dst_ref=rback.at[ex], send_sem=bs.at[to], recv_sem=br.at[ex],
            device_id=(to, dp), device_id_type=MESH,
        )

    def back_from(src):
        return pltpu.make_async_remote_copy(
            src_ref=sback.at[src], dst_ref=rback.at[src], send_sem=bs.at[src], recv_sem=br.at[src],
            device_id=(src, dp), device_id_type=MESH,
        )

    def others(first, last):
        return [(k, c) for k in range(first, last) for c in ((core, other) if k else (other,))]

    for k, c in others(0, n):
        forward(peer(k), c).start()
    recv[pl.ds(here, 1)] = send[pl.ds(here, 1)]

    def gather(first, count, xg):
        total = count * c_n
        for k in range(count):
            for c in range(c_n):
                src = source(first + k) * c_n + c
                i = k * c_n + c
                rows = recv[src, :, :width].astype(F32)
                xg[i * 8 : i * 8 + 8, :width] = rows[:8]
                xg[i * 8 : i * 8 + 8, width:] = rows[8:]
                tails_in[i * 16 : i * 16 + 16, :] = recv[src, :, width:]
        part = 2 * total
        r = lax.broadcasted_iota(jnp.int32, (8 * part, 1), 0)
        col = lax.broadcasted_iota(jnp.int32, (1, 8 * part), 1)
        wanted = ((r // 2) % total) * 16 + (r // part) * 2 + r % 2
        tails = nn(one_hot(wanted, col), tails_in[: 8 * part, :])
        for q in range(8):
            xg[8 * total : 10 * total, q * quarter : (q + 1) * quarter] = tails[q * part : q * part + part]
        spare = xg.shape[0] - 10 * total
        if spare:
            xg[10 * total :, :] = jnp.zeros((spare, 2 * width), F32)

    k0 = 0.7978845608028654
    k1 = 0.044715

    def multiply(xg, grow, to_x):
        f0 = pl.multiple_of(to_x * chunk, chunk)
        xa = xg[:, :width].astype(BF16)
        ga = xg[:, width:].astype(BF16)
        w1 = win[:, pl.ds(f0, chunk)]
        w2 = wout[pl.ds(f0, chunk), :]
        pre = nn(xa, w1)
        grad_hidden = nt(ga, w2)
        square = pre * pre
        th = jnp.tanh(k0 * pre * (1.0 + k1 * square))
        cdf = 0.5 * (1.0 + th)
        hidden = (pre * cdf).astype(BF16)
        slope = cdf + 0.5 * pre * (1.0 - th * th) * (k0 * (1.0 + 3.0 * k1 * square))
        grad_pre = (grad_hidden * slope).astype(BF16)
        grow[...] += nt(grad_pre, w1)
        return tn(hidden, ga)

    def give_back(first, count, grow):
        total = count * c_n
        small = grow[8 * total : 10 * total, :].astype(BF16)
        r = lax.broadcasted_iota(jnp.int32, (16 * count, 1), 0)
        col = lax.broadcasted_iota(jnp.int32, (1, 2 * total), 1)
        spread = nn(one_hot((r // 16) * 4 + r % 4, col), small)
        picked = spread[:, :quarter]
        for q in range(1, 4):
            picked = jnp.where((r // 4) % 4 == q, spread[:, q * quarter : (q + 1) * quarter], picked)
        picked = picked.astype(BF16)
        for k in range(count):
            to = source(first + k)
            sback[to, :, :width] = grow[k * 16 : k * 16 + 16, :].astype(BF16)
            sback[to, :, width:] = picked[k * 16 : k * 16 + 16]
            if first + k > 0:
                back_to(to).start()

    for k, c in others(0, near):
        forward_from(source(k), c).wait_recv()
    gather(0, near, xg_near)
    for copy in w_copies:
        copy.wait()
    grow_near[...] = jnp.zeros_like(grow_near)
    grow_far[...] = jnp.zeros_like(grow_far)

    def near_chunk(i, carry):
        to_x = (xx + 1 + i) % x_n
        acc[to_x] = multiply(xg_near, grow_near, to_x).reshape(zl_n, c_n, 16, width)
        return carry

    lax.fori_loop(0, x_n, near_chunk, 0)
    give_back(0, near, grow_near)
    rback[pl.ds(ex, 1)] = sback[pl.ds(ex, 1)]

    def to_x_copy(to_x):
        return pltpu.make_async_remote_copy(
            src_ref=xsend.at[to_x], dst_ref=xrecv.at[xx], send_sem=xs.at[to_x], recv_sem=xr.at[xx],
            device_id=(ex, dp_id(to_x, zl, core)), device_id_type=MESH,
        )

    def from_x_copy(src):
        return pltpu.make_async_remote_copy(
            src_ref=xsend.at[src], dst_ref=xrecv.at[src], send_sem=xs.at[src], recv_sem=xr.at[src],
            device_id=(ex, dp_id(src, zl, core)), device_id_type=MESH,
        )

    def z_copy(level):
        count = zl_n >> (level + 1)
        part = pl.ds(zl_n - 2 * count, count)
        return pltpu.make_async_remote_copy(
            src_ref=zsend.at[part], dst_ref=zrecv.at[part],
            send_sem=zs.at[level], recv_sem=zr.at[level],
            device_id=(ex, dp_id(xx, z_partner(level), core)), device_id_type=MESH,
        )

    def last_copy(at, to_z, to_c, sem):
        return pltpu.make_async_remote_copy(
            src_ref=zsend.at[at, to_c], dst_ref=zrecv.at[at, core],
            send_sem=zs.at[sem], recv_sem=zr.at[sem],
            device_id=(ex, dp_id(xx, to_z, to_c)), device_id_type=MESH,
        )

    def last_from(at, src_z, src_c, sem):
        return pltpu.make_async_remote_copy(
            src_ref=zsend.at[at, src_c], dst_ref=zrecv.at[at, src_c],
            send_sem=zs.at[sem], recv_sem=zr.at[sem],
            device_id=(ex, dp_id(xx, src_z, src_c)), device_id_type=MESH,
        )

    far_z = z_partner(levels - 1)
    last = [
        (zl_n - 2, far_z, core, levels - 1),
        (zl_n - 2, far_z, other, levels),
        (zl_n - 1, zl, other, levels + 1),
    ]

    for k, c in others(near, n):
        forward_from(source(k), c).wait_recv()
    gather(near, n - near, xg_far)

    def far_chunk(i, carry):
        to_x = (xx + 1 + i) % x_n
        term = multiply(xg_far, grow_far, to_x).reshape(zl_n, c_n, 16, width)
        xsend[to_x] = ((acc[to_x] + term) * scale).astype(BF16)
        to_x_copy(to_x).start()
        return carry

    lax.fori_loop(0, x_n - 1, far_chunk, 0)
    term = multiply(xg_far, grow_far, xx).reshape(zl_n, c_n, 16, width)
    acc[xx] = (acc[xx] + term) * scale
    give_back(near, n - near, grow_far)

    for k in range(1, x_n):
        from_x_copy((xx + x_n - k) % x_n).wait_recv()
    total = acc[xx]
    for k in range(1, x_n):
        total = total + xrecv[(xx + x_n - k) % x_n].astype(F32)
    acc[xx] = total
    for level in range(levels - 1):
        count = zl_n >> (level + 1)
        at = zl_n - 2 * count
        for m in range(count):
            zsend[at + m] = acc[xx, 2 * m + 1 - z_bit(level)].astype(BF16)
        z_copy(level).start()
        z_copy(level).wait_recv()
        for m in range(count):
            acc[xx, m] = acc[xx, 2 * m + z_bit(level)] + zrecv[at + m].astype(F32)
    zsend[zl_n - 2] = acc[xx, 1 - z_bit(levels - 1)].astype(BF16)
    zsend[zl_n - 1] = acc[xx, z_bit(levels - 1)].astype(BF16)
    for where in last:
        last_copy(*where).start()

    for k in range(1, n):
        back_from(peer(k)).wait_recv()
    back = rback[:, :, :width].astype(F32)
    first, second = back[:, :8], back[:, 8:]
    mine = core == 0
    dsend[...] = jnp.where(mine, second, first).reshape(8 * n, width).astype(BF16)
    tsend[...] = rback[:, :, width:].reshape(16 * n, quarter)

    def swap(which):
        src, dst = ((dsend, drecv), (tsend, trecv))[which]
        return pltpu.make_async_remote_copy(
            src_ref=src, dst_ref=dst, send_sem=ds.at[which], recv_sem=dr.at[which],
            device_id=(ex, dp_id(xx, zl, other)), device_id_type=MESH,
        )

    for which in range(2):
        swap(which).start()
    crow = lax.broadcasted_iota(jnp.int32, (8 * n, 1), 0)
    krow = lax.broadcasted_iota(jnp.int32, (16 * n, 1), 0)

    def collect(parity, rows, tail_rows):
        codes = (2 * (crow // 8) + parity) * CAP + crow % 8
        tail_codes = jnp.where(
            (krow // 2) % 2 == core, (2 * (krow // 16) + parity) * CAP + 8 + krow % 2, -2
        )
        wide = jnp.concatenate(
            [jnp.where((krow // 4) % 4 == q, tail_rows, 0.0) for q in range(4)], axis=1
        ).astype(BF16)
        return tn(one_hot(codes, code), rows) + tn(one_hot(tail_codes, code), wide)

    kept = jnp.where(mine, first, second).reshape(8 * n, width).astype(BF16)
    result = collect(core, kept, tsend[...].astype(F32))

    for where in last:
        last_from(*where).wait_recv()
    own = acc[xx, z_bit(levels - 1), core] + zrecv[zl_n - 2, core].astype(F32)
    cross = zrecv[zl_n - 1, other].astype(F32) + zrecv[zl_n - 2, other].astype(F32)
    gw_ref[:, 0, :] = jnp.where(mine, own, cross)
    gw_ref[:, 1, :] = jnp.where(mine, cross, own)

    for which in range(2):
        swap(which).wait_recv()
    gt_ref[...] = (result + collect(other, drecv[...], trecv[...].astype(F32))).astype(BF16)

    for k, c in others(0, n):
        forward(peer(k), c).wait_send()
    for k in range(1, n):
        back_to(source(k)).wait_send()
    for which in range(2):
        swap(which).wait_send()
    for k in range(1, x_n):
        to_x_copy((xx + k) % x_n).wait_send()
    for level in range(levels - 1):
        z_copy(level).wait_send()
    for where in last:
        last_copy(*where).wait_send()


def on_device(dims, tokens, cotangent, gates, expert_ids, slot_ids, w_in, w_out):
    zh_n, y_n, x_n, zl_n, c_n = dims
    n = zh_n * y_n
    rows, width = tokens.shape
    ff = w_in.shape[2]
    scale = 1.0 / math.sqrt(n * x_n * zl_n * c_n * CAP)
    experts = c_n * n
    near = n - y_n
    near_rows, far_rows = round_up(10 * near * c_n), round_up(10 * y_n * c_n)
    dma = pltpu.SemaphoreType.DMA
    hbm = pl.BlockSpec(memory_space=pltpu.HBM)
    vmem = pl.BlockSpec(memory_space=pltpu.VMEM)
    return pl.pallas_call(
        functools.partial(kernel, dims, scale),
        out_shape=(
            jax.ShapeDtypeStruct((rows, width), BF16),
            jax.ShapeDtypeStruct((ff // (x_n * zl_n * c_n), 2, width), F32),
        ),
        in_specs=[hbm] * 7,
        out_specs=(vmem, vmem),
        scratch_shapes=[
            pltpu.VMEM((rows, width), BF16),
            pltpu.VMEM((rows, width), BF16),
            pltpu.VMEM((1, rows), F32),
            pltpu.VMEM((1, rows), jnp.int32),
            pltpu.VMEM((1, rows), jnp.int32),
            pltpu.VMEM(w_in.shape[1:], BF16),
            pltpu.VMEM(w_out.shape[1:], BF16),
            pltpu.VMEM((experts, 16, width + width // 4), BF16),
            pltpu.VMEM((experts, 16, width + width // 4), BF16),
            pltpu.VMEM((near_rows, 2 * width), F32),
            pltpu.VMEM((far_rows, 2 * width), F32),
            pltpu.VMEM((16 * c_n * max(near, y_n), width // 4), BF16),
            pltpu.VMEM((near_rows, width), F32),
            pltpu.VMEM((far_rows, width), F32),
            pltpu.VMEM((n, 16, width + width // 4), BF16),
            pltpu.VMEM((n, 16, width + width // 4), BF16),
            pltpu.VMEM((8 * n, width), BF16),
            pltpu.VMEM((8 * n, width), BF16),
            pltpu.VMEM((16 * n, width // 4), BF16),
            pltpu.VMEM((16 * n, width // 4), BF16),
            pltpu.VMEM((x_n, zl_n, c_n, 16, width), F32),
            pltpu.VMEM((x_n, zl_n, c_n, 16, width), BF16),
            pltpu.VMEM((x_n, zl_n, c_n, 16, width), BF16),
            pltpu.VMEM((zl_n, c_n, 16, width), BF16),
            pltpu.VMEM((zl_n, c_n, 16, width), BF16),
            dma((5,)),
            dma((2,)),
            dma((experts,)),
            dma((experts,)),
            dma((n,)),
            dma((n,)),
            dma((2,)),
            dma((2,)),
            dma((x_n,)),
            dma((x_n,)),
            dma((zl_n.bit_length() + 1,)),
            dma((zl_n.bit_length() + 1,)),
        ],
        compiler_params=pltpu.CompilerParams(
            collective_id=0, has_side_effects=True, vmem_limit_bytes=60 << 20
        ),
        cost_estimate=pl.CostEstimate(
            flops=8 * CAP * experts * width * ff, bytes_accessed=6 << 20, transcendentals=CAP * experts * ff
        ),
        name="expert_backward",
    )(
        tokens, cotangent, gates.reshape(1, rows), expert_ids.reshape(1, rows),
        slot_ids.reshape(1, rows), w_in, w_out,
    )


def solution(mesh, dims=(ZH, Y, X, ZL, C)):
    return jax.shard_map(
        functools.partial(on_device, dims),
        mesh=mesh,
        in_specs=(
            P(("expert", "dp"), None),
            P(("expert", "dp"), None),
            P(("expert", "dp")),
            P(("expert", "dp")),
            P(("expert", "dp")),
            P("expert", None, None),
            P("expert", None, None),
        ),
        out_specs=(P(("expert", "dp"), None), P("dp", "expert", None)),
        check_vma=False,
    )
```

```python
import functools
import math

import jax
import jax.numpy as jnp
from jax import lax
from jax.experimental import pallas as pl
from jax.experimental.pallas import tpu as pltpu
from jax.sharding import PartitionSpec as P

MESH = pl.DeviceIdType.MESH
CAP = 10
F32 = jnp.float32
BF16 = jnp.bfloat16
ZH, Y, X, ZL, C = 4, 4, 4, 8, 2


def nn(a, b):
    return lax.dot_general(a, b, (((1,), (0,)), ((), ())), preferred_element_type=F32)


def nt(a, b):
    return lax.dot_general(a, b, (((1,), (1,)), ((), ())), preferred_element_type=F32)


def tn(a, b):
    return lax.dot_general(a, b, (((0,), (0,)), ((), ())), preferred_element_type=F32)


def one_hot(rows, cols):
    return jnp.where(rows == cols, 1.0, 0.0).astype(BF16)


def round_up(rows):
    return (rows + 15) // 16 * 16


def kernel(
    dims, scale,
    tok_hbm, cot_hbm, gate_hbm, eid_hbm, sid_hbm, win_hbm, wout_hbm,
    gt_ref, gw_ref,
    tok, cot, gate, eid, sid, win, wout, send, recv, xg_near, xg_far, tails_in, grow_near, grow_far,
    sback, rback, acc, own, csend, crecv, xsend, xrecv, zsend, zrecv,
    in_sem, w_sem, fs, fr, bs, br, cs, cr, xs, xr, zs, zr,
):
    zh_n, y_n, x_n, zl_n, c_n = dims
    n = zh_n * y_n
    tokens, width = tok.shape
    ff = win.shape[2]
    half = width // 2
    quarter = width // 4
    chunk = ff // x_n
    main = 16 * n

    ex = lax.axis_index("expert")
    dp = lax.axis_index("dp")
    zh, yy = ex // y_n, ex % y_n
    xx, zl, core = dp // (zl_n * c_n), (dp // c_n) % zl_n, dp % c_n
    other = 1 - core

    steps_z = sorted(range(zh_n), key=lambda dz: min(dz, zh_n - dz))
    offsets = [(dz, dy) for dz in steps_z for dy in range(y_n)]
    near = n - y_n

    def peer(k):
        dz, dy = offsets[k]
        return ((zh + dz) % zh_n) * y_n + (yy + dy) % y_n

    def source(k):
        dz, dy = offsets[k]
        return ((zh + zh_n - dz) % zh_n) * y_n + (yy + y_n - dy) % y_n

    def dp_id(a, b, c):
        return (a * zl_n + b) * c_n + c

    in_copies = [
        pltpu.make_async_copy(src, dst, in_sem.at[i])
        for i, (src, dst) in enumerate(
            [(eid_hbm, eid), (sid_hbm, sid), (gate_hbm, gate), (tok_hbm, tok), (cot_hbm, cot)]
        )
    ]
    w_copies = [
        pltpu.make_async_copy(win_hbm, win, w_sem.at[0]),
        pltpu.make_async_copy(wout_hbm, wout, w_sem.at[1]),
    ]
    for copy in in_copies + w_copies:
        copy.start()

    barrier = pltpu.get_barrier_semaphore()

    def greet(to_e, to_d):
        pl.semaphore_signal(barrier, inc=1, device_id=(to_e, to_d), device_id_type=MESH)

    for k in range(1, n):
        greet(peer(k), dp)
    greet(ex, dp_id(xx, zl, other))
    for k in range(1, x_n):
        greet(ex, dp_id((xx + k) % x_n, zl, core))
    for k in range(1, zl_n):
        greet(ex, dp_id(xx, (zl + k) % zl_n, core))

    for copy in in_copies[:3]:
        copy.wait()
    slot = sid[...]
    code = jnp.where(slot >= 0, eid[...] * CAP + slot, -1)
    row = lax.broadcasted_iota(jnp.int32, (main, 1), 0)
    main_code = (row // 8) * CAP + row % 8
    tail_block = (row // 4) % 4
    tail_code = (2 * (row // 16) + (row // 2) % 2) * CAP + 8 + row % 2
    t_main = one_hot(main_code, code)
    t_tail = one_hot(tail_code, code)
    gates = gate[...]
    gate_main = jnp.sum(jnp.where(main_code == code, gates, 0.0), axis=1, keepdims=True)
    gate_tail = jnp.sum(jnp.where(tail_code == code, gates, 0.0), axis=1, keepdims=True)

    for copy in in_copies[3:]:
        copy.wait()
    send[:, :, :width] = nn(t_main, tok[...]).astype(BF16).reshape(n, 16, width)
    send[:, :, width : 2 * width] = (
        (nn(t_main, cot[...]) * gate_main).astype(BF16).reshape(n, 16, width)
    )
    tail_x = nn(t_tail, tok[...])
    tail_g = nn(t_tail, cot[...]) * gate_tail
    tail = jnp.where(
        tail_block == 0,
        tail_x[:, :half],
        jnp.where(
            tail_block == 1,
            tail_x[:, half:],
            jnp.where(tail_block == 2, tail_g[:, :half], tail_g[:, half:]),
        ),
    )
    send[:, :, 2 * width :] = tail.astype(BF16).reshape(n, 16, half)

    pl.semaphore_wait(barrier, (n - 1) + 1 + (x_n - 1) + (zl_n - 1))

    def forward(to):
        return pltpu.make_async_remote_copy(
            src_ref=send.at[to], dst_ref=recv.at[ex], send_sem=fs.at[to], recv_sem=fr.at[ex],
            device_id=(to, dp), device_id_type=MESH,
        )

    def forward_from(src):
        return pltpu.make_async_remote_copy(
            src_ref=send.at[src], dst_ref=recv.at[src], send_sem=fs.at[src], recv_sem=fr.at[src],
            device_id=(src, dp), device_id_type=MESH,
        )

    def back_to(to):
        return pltpu.make_async_remote_copy(
            src_ref=sback.at[to], dst_ref=rback.at[ex], send_sem=bs.at[to], recv_sem=br.at[ex],
            device_id=(to, dp), device_id_type=MESH,
        )

    def back_from(src):
        return pltpu.make_async_remote_copy(
            src_ref=sback.at[src], dst_ref=rback.at[src], send_sem=bs.at[src], recv_sem=br.at[src],
            device_id=(src, dp), device_id_type=MESH,
        )

    for k in range(1, n):
        forward(peer(k)).start()
    recv[pl.ds(ex, 1)] = send[pl.ds(ex, 1)]

    def gather(first, count, xg):
        for k in range(count):
            src = source(first + k)
            block = recv[src, :, : 2 * width].astype(F32)
            xg[0, k * 8 : k * 8 + 8, :] = block[:8]
            xg[1, k * 8 : k * 8 + 8, :] = block[8:]
            tails_in[k * 16 : k * 16 + 16, :] = recv[src, :, 2 * width :]
        part = 2 * count
        r = lax.broadcasted_iota(jnp.int32, (8 * part, 1), 0)
        col = lax.broadcasted_iota(jnp.int32, (1, 8 * part), 1)
        wanted = (
            ((r // 2) % count) * 16
            + ((r // part) % 4) * 4
            + (r // (4 * part)) * 2
            + r % 2
        )
        tails = nn(one_hot(wanted, col), tails_in[: 8 * part, :])
        for a in range(2):
            for q in range(4):
                at = (a * 4 + q) * part
                xg[a, 8 * count : 10 * count, q * half : (q + 1) * half] = tails[at : at + part]
            spare = xg.shape[1] - 10 * count
            if spare:
                xg[a, 10 * count :, :] = jnp.zeros((spare, 2 * width), F32)

    k0 = 0.7978845608028654
    k1 = 0.044715

    def place(i):
        return i // x_n, (xx + 1 + i % x_n) % x_n

    def multiply(xg, grow, i):
        a, to_x = place(i)
        f0 = pl.multiple_of(to_x * chunk, chunk)
        xa = xg[a, :, :width].astype(BF16)
        ga = xg[a, :, width:].astype(BF16)
        w1 = win[a, :, pl.ds(f0, chunk)]
        w2 = wout[a, pl.ds(f0, chunk), :]
        pre = nn(xa, w1)
        grad_hidden = nt(ga, w2)
        square = pre * pre
        th = jnp.tanh(k0 * pre * (1.0 + k1 * square))
        cdf = 0.5 * (1.0 + th)
        hidden = (pre * cdf).astype(BF16)
        slope = cdf + 0.5 * pre * (1.0 - th * th) * (k0 * (1.0 + 3.0 * k1 * square))
        grad_pre = (grad_hidden * slope).astype(BF16)
        grow[a] += nt(grad_pre, w1)
        return tn(hidden, ga)

    def give_back(first, count, grow):
        for k in range(count):
            both = jnp.concatenate(
                [grow[0, k * 8 : k * 8 + 8, :], grow[1, k * 8 : k * 8 + 8, :]], axis=0
            )
            sback[source(first + k), :, :width] = both.astype(BF16)
        part = 2 * count
        small = jnp.concatenate(
            [grow[0, 8 * count : 10 * count, :], grow[1, 8 * count : 10 * count, :]], axis=0
        ).astype(BF16)
        r = lax.broadcasted_iota(jnp.int32, (16 * count, 1), 0)
        col = lax.broadcasted_iota(jnp.int32, (1, 2 * part), 1)
        spread = nn(one_hot(((r // 2) % 2) * part + (r // 16) * 2 + r % 2, col), small)
        block = (r // 4) % 4
        cols = [spread[:, q * quarter : (q + 1) * quarter] for q in range(4)]
        picked = jnp.where(
            block == 0, cols[0], jnp.where(block == 1, cols[1], jnp.where(block == 2, cols[2], cols[3]))
        ).astype(BF16)
        for k in range(count):
            sback[source(first + k), :, width:] = picked[k * 16 : k * 16 + 16]
            if first + k > 0:
                back_to(source(first + k)).start()

    for k in range(1, near):
        forward_from(source(k)).wait_recv()
    gather(0, near, xg_near)
    for copy in w_copies:
        copy.wait()
    grow_near[...] = jnp.zeros_like(grow_near)
    grow_far[...] = jnp.zeros_like(grow_far)

    def near_chunk(i, carry):
        a, to_x = place(i)
        acc[a, to_x] = multiply(xg_near, grow_near, i).reshape(zl_n, c_n, 16, width)
        return carry

    lax.fori_loop(0, 2 * x_n, near_chunk, 0)
    give_back(0, near, grow_near)
    rback[pl.ds(ex, 1)] = sback[pl.ds(ex, 1)]

    def to_core(a, to_x):
        return pltpu.make_async_remote_copy(
            src_ref=csend.at[a, to_x], dst_ref=crecv.at[a, to_x],
            send_sem=cs.at[a, to_x], recv_sem=cr.at[a, to_x],
            device_id=(ex, dp_id(xx, zl, other)), device_id_type=MESH,
        )

    def to_x_copy(a, to_x):
        return pltpu.make_async_remote_copy(
            src_ref=xsend.at[a, to_x], dst_ref=xrecv.at[a, xx],
            send_sem=xs.at[a, to_x], recv_sem=xr.at[a, xx],
            device_id=(ex, dp_id(to_x, zl, core)), device_id_type=MESH,
        )

    def from_x_copy(a, src):
        return pltpu.make_async_remote_copy(
            src_ref=xsend.at[a, src], dst_ref=xrecv.at[a, src],
            send_sem=xs.at[a, src], recv_sem=xr.at[a, src],
            device_id=(ex, dp_id(src, zl, core)), device_id_type=MESH,
        )

    def to_z_copy(a, to_z):
        return pltpu.make_async_remote_copy(
            src_ref=zsend.at[a, to_z], dst_ref=zrecv.at[a, zl],
            send_sem=zs.at[a, to_z], recv_sem=zr.at[a, zl],
            device_id=(ex, dp_id(xx, to_z, core)), device_id_type=MESH,
        )

    def from_z_copy(a, src):
        return pltpu.make_async_remote_copy(
            src_ref=zsend.at[a, src], dst_ref=zrecv.at[a, src],
            send_sem=zs.at[a, src], recv_sem=zr.at[a, src],
            device_id=(ex, dp_id(xx, src, core)), device_id_type=MESH,
        )

    def far_chunk(i):
        a, to_x = place(i)
        term = (acc[a, to_x] + multiply(xg_far, grow_far, i).reshape(zl_n, c_n, 16, width)) * scale
        even, odd = term[:, 0], term[:, 1]
        mine = core == 0
        own[a, to_x] = jnp.where(mine, even, odd)
        csend[a, to_x] = jnp.where(mine, odd, even).astype(BF16)
        to_core(a, to_x).start()

    def far_first(i, carry):
        far_chunk(i)
        return carry

    def pass_x(i):
        a, to_x = place(i)
        to_core(a, to_x).wait_recv()
        xsend[a, to_x] = (own[a, to_x] + crecv[a, to_x].astype(F32)).astype(BF16)
        to_x_copy(a, to_x).start()

    def far_next(i, carry):
        far_chunk(i)
        pass_x(i - 2)
        return carry

    for k in range(near, n):
        forward_from(source(k)).wait_recv()
    gather(near, n - near, xg_far)
    lax.fori_loop(0, 2, far_first, 0)
    lax.fori_loop(2, x_n + 1, far_next, 0)
    far_chunk(x_n + 1)
    lax.fori_loop(x_n + 2, 2 * x_n, far_next, 0)
    pass_x(2 * x_n - 2)
    give_back(near, n - near, grow_far)

    for a in range(2):
        to_core(a, xx).wait_recv()
        own[a, xx] += crecv[a, xx].astype(F32)
    for a in range(2):
        for k in range(1, x_n):
            src = (xx + x_n - k) % x_n
            from_x_copy(a, src).wait_recv()
            own[a, xx] += xrecv[a, src].astype(F32)
        zsend[a] = own[a, xx].astype(BF16)
        for k in range(1, zl_n):
            to_z_copy(a, (zl + k) % zl_n).start()

    for k in range(1, n):
        back_from(peer(k)).wait_recv()
    back_main = rback[:, :, :width].reshape(main, width)
    back_tail = rback[:, :, width:].reshape(main, quarter).astype(F32)
    wide = jnp.concatenate(
        [jnp.where(tail_block == q, back_tail, 0.0) for q in range(4)], axis=1
    ).astype(BF16)
    gt_ref[...] = (tn(t_main, back_main) + tn(t_tail, wide)).astype(BF16)

    for a in range(2):
        total = own[a, xx, zl]
        for k in range(1, zl_n):
            src = (zl + k) % zl_n
            from_z_copy(a, src).wait_recv()
            total = total + zrecv[a, src].astype(F32)
        gw_ref[:, a, :] = total

    for k in range(1, n):
        forward(peer(k)).wait_send()
        back_to(source(k)).wait_send()
    for a in range(2):
        for k in range(x_n):
            to_core(a, (xx + k) % x_n).wait_send()
        for k in range(1, x_n):
            to_x_copy(a, (xx + k) % x_n).wait_send()
        for k in range(1, zl_n):
            to_z_copy(a, (zl + k) % zl_n).wait_send()


def on_device(dims, tokens, cotangent, gates, expert_ids, slot_ids, w_in, w_out):
    zh_n, y_n, x_n, zl_n, c_n = dims
    n = zh_n * y_n
    rows, width = tokens.shape
    ff = w_in.shape[2]
    scale = 1.0 / math.sqrt(n * x_n * zl_n * c_n * CAP)
    per = 10 * n
    near = n - y_n
    near_rows, far_rows = round_up(10 * near), round_up(10 * y_n)
    dma = pltpu.SemaphoreType.DMA
    hbm = pl.BlockSpec(memory_space=pltpu.HBM)
    vmem = pl.BlockSpec(memory_space=pltpu.VMEM)
    return pl.pallas_call(
        functools.partial(kernel, dims, scale),
        out_shape=(
            jax.ShapeDtypeStruct((rows, width), BF16),
            jax.ShapeDtypeStruct((ff // (x_n * zl_n * c_n), 2, width), F32),
        ),
        in_specs=[hbm] * 7,
        out_specs=(vmem, vmem),
        scratch_shapes=[
            pltpu.VMEM((rows, width), BF16),
            pltpu.VMEM((rows, width), BF16),
            pltpu.VMEM((1, rows), F32),
            pltpu.VMEM((1, rows), jnp.int32),
            pltpu.VMEM((1, rows), jnp.int32),
            pltpu.VMEM(w_in.shape, BF16),
            pltpu.VMEM(w_out.shape, BF16),
            pltpu.VMEM((n, 16, 2 * width + width // 2), BF16),
            pltpu.VMEM((n, 16, 2 * width + width // 2), BF16),
            pltpu.VMEM((2, near_rows, 2 * width), F32),
            pltpu.VMEM((2, far_rows, 2 * width), F32),
            pltpu.VMEM((16 * max(near, y_n), width // 2), BF16),
            pltpu.VMEM((2, near_rows, width), F32),
            pltpu.VMEM((2, far_rows, width), F32),
            pltpu.VMEM((n, 16, width + width // 4), BF16),
            pltpu.VMEM((n, 16, width + width // 4), BF16),
            pltpu.VMEM((2, x_n, zl_n, c_n, 16, width), F32),
            pltpu.VMEM((2, x_n, zl_n, 16, width), F32),
            pltpu.VMEM((2, x_n, zl_n, 16, width), BF16),
            pltpu.VMEM((2, x_n, zl_n, 16, width), BF16),
            pltpu.VMEM((2, x_n, zl_n, 16, width), BF16),
            pltpu.VMEM((2, x_n, zl_n, 16, width), BF16),
            pltpu.VMEM((2, zl_n, 16, width), BF16),
            pltpu.VMEM((2, zl_n, 16, width), BF16),
            dma((5,)),
            dma((2,)),
            dma((n,)),
            dma((n,)),
            dma((n,)),
            dma((n,)),
            dma((2, x_n)),
            dma((2, x_n)),
            dma((2, x_n)),
            dma((2, x_n)),
            dma((2, zl_n)),
            dma((2, zl_n)),
        ],
        compiler_params=pltpu.CompilerParams(
            collective_id=0, has_side_effects=True, vmem_limit_bytes=60 << 20
        ),
        cost_estimate=pl.CostEstimate(
            flops=8 * 2 * per * width * ff, bytes_accessed=6 << 20, transcendentals=2 * per * ff
        ),
        name="expert_backward",
    )(
        tokens, cotangent, gates.reshape(1, rows), expert_ids.reshape(1, rows),
        slot_ids.reshape(1, rows), w_in, w_out,
    )


def solution(mesh, dims=(ZH, Y, X, ZL, C)):
    return jax.shard_map(
        functools.partial(on_device, dims),
        mesh=mesh,
        in_specs=(
            P(("expert", "dp"), None),
            P(("expert", "dp"), None),
            P(("expert", "dp")),
            P(("expert", "dp")),
            P(("expert", "dp")),
            P("expert", None, None),
            P("expert", None, None),
        ),
        out_specs=(P(("expert", "dp"), None), P("dp", "expert", None)),
        check_vma=False,
    )
```

```python
import functools
import math

import jax
import jax.numpy as jnp
from jax import lax
from jax.experimental import pallas as pl
from jax.experimental.pallas import tpu as pltpu
from jax.sharding import PartitionSpec as P

MESH = pl.DeviceIdType.MESH
CAP = 10
F32 = jnp.float32
BF16 = jnp.bfloat16
ZH, Y, X, ZL, C = 4, 4, 4, 8, 2


def nn(a, b):
    return lax.dot_general(a, b, (((1,), (0,)), ((), ())), preferred_element_type=F32)


def nt(a, b):
    return lax.dot_general(a, b, (((1,), (1,)), ((), ())), preferred_element_type=F32)


def tn(a, b):
    return lax.dot_general(a, b, (((0,), (0,)), ((), ())), preferred_element_type=F32)


def one_hot(rows, cols):
    return jnp.where(rows == cols, 1.0, 0.0).astype(BF16)


def round_up(rows):
    return (rows + 15) // 16 * 16


def kernel(
    dims, scale,
    tok_hbm, cot_hbm, route_ref, win_hbm, wout_hbm,
    gt_ref, gw_ref,
    tok, cot, win, wout, send, recv, xg_near, xg_far, tails_in, grow_near, grow_far,
    sback, rback, acc, own, csend, crecv, xsend, xrecv, zsend, zrecv,
    in_sem, w_sem, fs, fr, bs, br, cs, cr, xs, xr, zs, zr,
):
    zh_n, y_n, x_n, zl_n, c_n = dims
    n = zh_n * y_n
    tokens, width = tok.shape
    ff = win.shape[2]
    half = width // 2
    quarter = width // 4
    chunk = ff // x_n
    main = 16 * n

    ex = lax.axis_index("expert")
    dp = lax.axis_index("dp")
    zh, yy = ex // y_n, ex % y_n
    xx, zl, core = dp // (zl_n * c_n), (dp // c_n) % zl_n, dp % c_n
    other = 1 - core

    steps_z = sorted(range(zh_n), key=lambda dz: min(dz, zh_n - dz))
    offsets = [(dz, dy) for dz in steps_z for dy in range(y_n)]
    near = n - y_n

    def peer(k):
        dz, dy = offsets[k]
        return ((zh + dz) % zh_n) * y_n + (yy + dy) % y_n

    def source(k):
        dz, dy = offsets[k]
        return ((zh + zh_n - dz) % zh_n) * y_n + (yy + y_n - dy) % y_n

    def dp_id(a, b, c):
        return (a * zl_n + b) * c_n + c

    in_copies = [
        pltpu.make_async_copy(src, dst, in_sem.at[i])
        for i, (src, dst) in enumerate(
            [(tok_hbm, tok), (cot_hbm, cot)]
        )
    ]
    w_copies = [
        pltpu.make_async_copy(win_hbm, win, w_sem.at[0]),
        pltpu.make_async_copy(wout_hbm, wout, w_sem.at[1]),
    ]
    for copy in in_copies + w_copies:
        copy.start()

    barrier = pltpu.get_barrier_semaphore()

    def greet(to_e, to_d):
        pl.semaphore_signal(barrier, inc=1, device_id=(to_e, to_d), device_id_type=MESH)

    for k in range(1, n):
        greet(peer(k), dp)
    greet(ex, dp_id(xx, zl, other))
    for k in range(1, x_n):
        greet(ex, dp_id((xx + k) % x_n, zl, core))
    for k in range(1, zl_n):
        greet(ex, dp_id(xx, (zl + k) % zl_n, core))

    slot = route_ref[2:3, :].astype(jnp.int32)
    code = jnp.where(slot >= 0, route_ref[1:2, :].astype(jnp.int32) * CAP + slot, -1)
    row = lax.broadcasted_iota(jnp.int32, (main, 1), 0)
    main_code = (row // 8) * CAP + row % 8
    tail_block = (row // 4) % 4
    tail_code = (2 * (row // 16) + (row // 2) % 2) * CAP + 8 + row % 2
    t_main = one_hot(main_code, code)
    t_tail = one_hot(tail_code, code)
    gates = route_ref[0:1, :]
    gate_main = jnp.sum(jnp.where(main_code == code, gates, 0.0), axis=1, keepdims=True)
    gate_tail = jnp.sum(jnp.where(tail_code == code, gates, 0.0), axis=1, keepdims=True)

    for copy in in_copies:
        copy.wait()
    send[:, :, :width] = nn(t_main, tok[...]).astype(BF16).reshape(n, 16, width)
    send[:, :, width : 2 * width] = (
        (nn(t_main, cot[...]) * gate_main).astype(BF16).reshape(n, 16, width)
    )
    tail_x = nn(t_tail, tok[...])
    tail_g = nn(t_tail, cot[...]) * gate_tail
    tail = jnp.where(
        tail_block == 0,
        tail_x[:, :half],
        jnp.where(
            tail_block == 1,
            tail_x[:, half:],
            jnp.where(tail_block == 2, tail_g[:, :half], tail_g[:, half:]),
        ),
    )
    send[:, :, 2 * width :] = tail.astype(BF16).reshape(n, 16, half)

    pl.semaphore_wait(barrier, (n - 1) + 1 + (x_n - 1) + (zl_n - 1))

    def forward(to):
        return pltpu.make_async_remote_copy(
            src_ref=send.at[to], dst_ref=recv.at[ex], send_sem=fs.at[to], recv_sem=fr.at[ex],
            device_id=(to, dp), device_id_type=MESH,
        )

    def forward_from(src):
        return pltpu.make_async_remote_copy(
            src_ref=send.at[src], dst_ref=recv.at[src], send_sem=fs.at[src], recv_sem=fr.at[src],
            device_id=(src, dp), device_id_type=MESH,
        )

    def back_to(to):
        return pltpu.make_async_remote_copy(
            src_ref=sback.at[to], dst_ref=rback.at[ex], send_sem=bs.at[to], recv_sem=br.at[ex],
            device_id=(to, dp), device_id_type=MESH,
        )

    def back_from(src):
        return pltpu.make_async_remote_copy(
            src_ref=sback.at[src], dst_ref=rback.at[src], send_sem=bs.at[src], recv_sem=br.at[src],
            device_id=(src, dp), device_id_type=MESH,
        )

    for k in range(1, n):
        forward(peer(k)).start()
    recv[pl.ds(ex, 1)] = send[pl.ds(ex, 1)]

    def gather(first, count, xg):
        for k in range(count):
            src = source(first + k)
            block = recv[src, :, : 2 * width].astype(F32)
            xg[0, k * 8 : k * 8 + 8, :] = block[:8]
            xg[1, k * 8 : k * 8 + 8, :] = block[8:]
            tails_in[k * 16 : k * 16 + 16, :] = recv[src, :, 2 * width :]
        part = 2 * count
        r = lax.broadcasted_iota(jnp.int32, (8 * part, 1), 0)
        col = lax.broadcasted_iota(jnp.int32, (1, 8 * part), 1)
        wanted = (
            ((r // 2) % count) * 16
            + ((r // part) % 4) * 4
            + (r // (4 * part)) * 2
            + r % 2
        )
        tails = nn(one_hot(wanted, col), tails_in[: 8 * part, :])
        for a in range(2):
            for q in range(4):
                at = (a * 4 + q) * part
                xg[a, 8 * count : 10 * count, q * half : (q + 1) * half] = tails[at : at + part]
            spare = xg.shape[1] - 10 * count
            if spare:
                xg[a, 10 * count :, :] = jnp.zeros((spare, 2 * width), F32)

    k0 = 0.7978845608028654
    k1 = 0.044715

    def place(i):
        return i % 2, (xx + 1 + i // 2) % x_n

    def multiply(xg, grow, i):
        a, to_x = place(i)
        f0 = pl.multiple_of(to_x * chunk, chunk)
        xa = xg[a, :, :width].astype(BF16)
        ga = xg[a, :, width:].astype(BF16)
        w1 = win[a, :, pl.ds(f0, chunk)]
        w2 = wout[a, pl.ds(f0, chunk), :]
        pre = nn(xa, w1)
        grad_hidden = nt(ga, w2)
        square = pre * pre
        th = jnp.tanh(k0 * pre * (1.0 + k1 * square))
        cdf = 0.5 * (1.0 + th)
        hidden = (pre * cdf).astype(BF16)
        slope = cdf + 0.5 * pre * (1.0 - th * th) * (k0 * (1.0 + 3.0 * k1 * square))
        grad_pre = (grad_hidden * slope).astype(BF16)
        grow[a] += nt(grad_pre, w1)
        return tn(hidden, ga)

    def give_back(first, count, grow):
        for k in range(count):
            both = jnp.concatenate(
                [grow[0, k * 8 : k * 8 + 8, :], grow[1, k * 8 : k * 8 + 8, :]], axis=0
            )
            sback[source(first + k), :, :width] = both.astype(BF16)
        part = 2 * count
        small = jnp.concatenate(
            [grow[0, 8 * count : 10 * count, :], grow[1, 8 * count : 10 * count, :]], axis=0
        ).astype(BF16)
        r = lax.broadcasted_iota(jnp.int32, (16 * count, 1), 0)
        col = lax.broadcasted_iota(jnp.int32, (1, 2 * part), 1)
        spread = nn(one_hot(((r // 2) % 2) * part + (r // 16) * 2 + r % 2, col), small)
        block = (r // 4) % 4
        cols = [spread[:, q * quarter : (q + 1) * quarter] for q in range(4)]
        picked = jnp.where(
            block == 0, cols[0], jnp.where(block == 1, cols[1], jnp.where(block == 2, cols[2], cols[3]))
        ).astype(BF16)
        for k in range(count):
            sback[source(first + k), :, width:] = picked[k * 16 : k * 16 + 16]
            if first + k > 0:
                back_to(source(first + k)).start()

    for k in range(1, near):
        forward_from(source(k)).wait_recv()
    gather(0, near, xg_near)
    for copy in w_copies:
        copy.wait()
    grow_near[...] = jnp.zeros_like(grow_near)
    grow_far[...] = jnp.zeros_like(grow_far)

    def near_chunk(i, carry):
        a, to_x = place(i)
        acc[a, to_x] = multiply(xg_near, grow_near, i).reshape(zl_n, c_n, 16, width)
        return carry

    lax.fori_loop(0, 2 * x_n, near_chunk, 0)
    give_back(0, near, grow_near)
    rback[pl.ds(ex, 1)] = sback[pl.ds(ex, 1)]

    def to_core(a, to_x):
        return pltpu.make_async_remote_copy(
            src_ref=csend.at[a, to_x], dst_ref=crecv.at[a, to_x],
            send_sem=cs.at[a, to_x], recv_sem=cr.at[a, to_x],
            device_id=(ex, dp_id(xx, zl, other)), device_id_type=MESH,
        )

    def to_x_copy(a, to_x):
        return pltpu.make_async_remote_copy(
            src_ref=xsend.at[a, to_x], dst_ref=xrecv.at[a, xx],
            send_sem=xs.at[a, to_x], recv_sem=xr.at[a, xx],
            device_id=(ex, dp_id(to_x, zl, core)), device_id_type=MESH,
        )

    def from_x_copy(a, src):
        return pltpu.make_async_remote_copy(
            src_ref=xsend.at[a, src], dst_ref=xrecv.at[a, src],
            send_sem=xs.at[a, src], recv_sem=xr.at[a, src],
            device_id=(ex, dp_id(src, zl, core)), device_id_type=MESH,
        )

    def to_z_copy(a, to_z):
        return pltpu.make_async_remote_copy(
            src_ref=zsend.at[a, to_z], dst_ref=zrecv.at[a, zl],
            send_sem=zs.at[a, to_z], recv_sem=zr.at[a, zl],
            device_id=(ex, dp_id(xx, to_z, core)), device_id_type=MESH,
        )

    def from_z_copy(a, src):
        return pltpu.make_async_remote_copy(
            src_ref=zsend.at[a, src], dst_ref=zrecv.at[a, src],
            send_sem=zs.at[a, src], recv_sem=zr.at[a, src],
            device_id=(ex, dp_id(xx, src, core)), device_id_type=MESH,
        )

    def far_chunk(i):
        a, to_x = place(i)
        term = (acc[a, to_x] + multiply(xg_far, grow_far, i).reshape(zl_n, c_n, 16, width)) * scale
        even, odd = term[:, 0], term[:, 1]
        mine = core == 0
        own[a, to_x] = jnp.where(mine, even, odd)
        csend[a, to_x] = jnp.where(mine, odd, even).astype(BF16)
        to_core(a, to_x).start()

    def far_first(i, carry):
        far_chunk(i)
        return carry

    def far_next(i, carry):
        far_chunk(i)
        a, to_x = place(i - 2)
        to_core(a, to_x).wait_recv()
        xsend[a, to_x] = (own[a, to_x] + crecv[a, to_x].astype(F32)).astype(BF16)
        to_x_copy(a, to_x).start()
        return carry

    for k in range(near, n):
        forward_from(source(k)).wait_recv()
    gather(near, n - near, xg_far)
    lax.fori_loop(0, 2, far_first, 0)
    lax.fori_loop(2, 2 * x_n, far_next, 0)
    give_back(near, n - near, grow_far)

    for a in range(2):
        to_core(a, xx).wait_recv()
        own[a, xx] += crecv[a, xx].astype(F32)
    for a in range(2):
        for k in range(1, x_n):
            src = (xx + x_n - k) % x_n
            from_x_copy(a, src).wait_recv()
            own[a, xx] += xrecv[a, src].astype(F32)
        zsend[a] = own[a, xx].astype(BF16)
        for k in range(1, zl_n):
            to_z_copy(a, (zl + k) % zl_n).start()

    for k in range(1, n):
        back_from(peer(k)).wait_recv()
    back_main = rback[:, :, :width].reshape(main, width)
    back_tail = rback[:, :, width:].reshape(main, quarter).astype(F32)
    wide = jnp.concatenate(
        [jnp.where(tail_block == q, back_tail, 0.0) for q in range(4)], axis=1
    ).astype(BF16)
    gt_ref[...] = (tn(t_main, back_main) + tn(t_tail, wide)).astype(BF16)

    for a in range(2):
        total = own[a, xx, zl]
        for k in range(1, zl_n):
            src = (zl + k) % zl_n
            from_z_copy(a, src).wait_recv()
            total = total + zrecv[a, src].astype(F32)
        gw_ref[:, a, :] = total

    for k in range(1, n):
        forward(peer(k)).wait_send()
        back_to(source(k)).wait_send()
    for a in range(2):
        for k in range(x_n):
            to_core(a, (xx + k) % x_n).wait_send()
        for k in range(1, x_n):
            to_x_copy(a, (xx + k) % x_n).wait_send()
        for k in range(1, zl_n):
            to_z_copy(a, (zl + k) % zl_n).wait_send()


def on_device(dims, tokens, cotangent, gates, expert_ids, slot_ids, w_in, w_out):
    zh_n, y_n, x_n, zl_n, c_n = dims
    n = zh_n * y_n
    rows, width = tokens.shape
    ff = w_in.shape[2]
    scale = 1.0 / math.sqrt(n * x_n * zl_n * c_n * CAP)
    per = 10 * n
    near = n - y_n
    near_rows, far_rows = round_up(10 * near), round_up(10 * y_n)
    dma = pltpu.SemaphoreType.DMA
    hbm = pl.BlockSpec(memory_space=pltpu.HBM)
    vmem = pl.BlockSpec(memory_space=pltpu.VMEM)
    return pl.pallas_call(
        functools.partial(kernel, dims, scale),
        out_shape=(
            jax.ShapeDtypeStruct((rows, width), BF16),
            jax.ShapeDtypeStruct((ff // (x_n * zl_n * c_n), 2, width), F32),
        ),
        in_specs=[hbm, hbm, vmem, hbm, hbm],
        out_specs=(vmem, vmem),
        scratch_shapes=[
            pltpu.VMEM((rows, width), BF16),
            pltpu.VMEM((rows, width), BF16),
            pltpu.VMEM(w_in.shape, BF16),
            pltpu.VMEM(w_out.shape, BF16),
            pltpu.VMEM((n, 16, 2 * width + width // 2), BF16),
            pltpu.VMEM((n, 16, 2 * width + width // 2), BF16),
            pltpu.VMEM((2, near_rows, 2 * width), F32),
            pltpu.VMEM((2, far_rows, 2 * width), F32),
            pltpu.VMEM((16 * max(near, y_n), width // 2), BF16),
            pltpu.VMEM((2, near_rows, width), F32),
            pltpu.VMEM((2, far_rows, width), F32),
            pltpu.VMEM((n, 16, width + width // 4), BF16),
            pltpu.VMEM((n, 16, width + width // 4), BF16),
            pltpu.VMEM((2, x_n, zl_n, c_n, 16, width), F32),
            pltpu.VMEM((2, x_n, zl_n, 16, width), F32),
            pltpu.VMEM((2, x_n, zl_n, 16, width), BF16),
            pltpu.VMEM((2, x_n, zl_n, 16, width), BF16),
            pltpu.VMEM((2, x_n, zl_n, 16, width), BF16),
            pltpu.VMEM((2, x_n, zl_n, 16, width), BF16),
            pltpu.VMEM((2, zl_n, 16, width), BF16),
            pltpu.VMEM((2, zl_n, 16, width), BF16),
            dma((2,)),
            dma((2,)),
            dma((n,)),
            dma((n,)),
            dma((n,)),
            dma((n,)),
            dma((2, x_n)),
            dma((2, x_n)),
            dma((2, x_n)),
            dma((2, x_n)),
            dma((2, zl_n)),
            dma((2, zl_n)),
        ],
        compiler_params=pltpu.CompilerParams(
            collective_id=0, has_side_effects=True, vmem_limit_bytes=(53 << 20) + (1 << 19)
        ),
        cost_estimate=pl.CostEstimate(
            flops=8 * 2 * per * width * ff, bytes_accessed=6 << 20, transcendentals=2 * per * ff
        ),
        name="expert_backward",
    )(
        tokens, cotangent, jnp.stack([gates, expert_ids.astype(F32), slot_ids.astype(F32)]),
        w_in, w_out,
    )


def solution(mesh, dims=(ZH, Y, X, ZL, C)):
    return jax.shard_map(
        functools.partial(on_device, dims),
        mesh=mesh,
        in_specs=(
            P(("expert", "dp"), None),
            P(("expert", "dp"), None),
            P(("expert", "dp")),
            P(("expert", "dp")),
            P(("expert", "dp")),
            P("expert", None, None),
            P("expert", None, None),
        ),
        out_specs=(P(("expert", "dp"), None), P("dp", "expert", None)),
        check_vma=False,
    )
```
